128 devices in a mesh: gx: 8 (over z, core), gy: 16 (over y, x).
Axes of the slice: x: 4, y: 4, z: 4, core: 2. Of those that a mesh axis runs over, the one named last changes fastest.
Arguments:
- old_state: float32 [8, 128, 3, 128, 128], P('gx', 'gy'), as said below
- old_dest: int32 [8, 128], P('gx', 'gy'), may hold values from -1 to 127, as said below
- refine: int32 [8, 128], P('gx', 'gy'), may hold values from 0 to 1, as said below
- parent_block: int32 [8, 128], P('gx', 'gy'), may hold values from 0 to 63, as said below
- coarse_state: float32 [16, 16, 3, 128, 128], P('gx', 'gy'), as said below
- force: float32 [2, 1024, 16384], P(None, 'gx', 'gy'), may hold values from -6 to 6
Outputs:
- depth_out: float32 [1024, 16384], P('gx', 'gy')
- velocity_out: float32 [2, 1024, 16384], P(None, 'gx', 'gy')
The draws below stay inside these ranges and needn't reach their ends.
Inputs may be any that keep to these rules, and one draw needn't show every extreme that they name: `old_state`: channel 0 of each patch is the water depth, between 0.5 and 2. `coarse_state`: channel 0 of each patch is the water depth, between 0.5 and 2. `old_dest`: A new column is device times 8 plus position within the device, in the same gx row. The slots of one device go to different devices, at most one to each device of its gy row; every position whose refine is 0 receives exactly one slot, a refined one none. In one gx row, the slot at a given position within its device goes the same number of devices onward along gy (modulo 16) on every device, or is -1. `refine`: A device holds at most 2 refined patches; in every gx row some device holds exactly 2. `parent_block`: the parents of all patches of one device lie on one device of its gy column. Quadrant 0 is low first and low second index, 1 low and high, 2 high and low, 3 high and high.
All inputs are finite; a program needn't handle non-finite values.
Results may differ from the reference program's by a relative error of at most 0.0003.
Values sent between devices are 32-bit elements; how exact they have to be, the bound alone decides.
No kernel may reach another device: no remote copies, remote signals or barrier semaphores. Data moves between devices by JAX's collectives and lax.ppermute only.
A program may use at most 64 MiB of HBM per device.

```python
import jax
import jax.numpy as jnp
from jax import lax

CELLS = 128
FIELDS = 3
P_DEV = 8
C_DEV = 2
SWEEPS = 6
RMOST = 2
NX = 1024
NY = 16384
N_GX = 8
N_GY = 16


def plan_tables(key):
    key_list = jax.random.split(key, 7)
    columns = N_GY * P_DEV
    device_ids = jnp.arange(N_GY, dtype=jnp.int32)
    slot_ids = jnp.arange(P_DEV, dtype=jnp.int32)
    row_ids = jnp.arange(N_GX, dtype=jnp.int32)[:, None, None]
    offset_score = jax.random.randint(key_list[0], (N_GX, N_GY), 0, 1 << 20) * N_GY + device_ids[None, :]
    offsets = jnp.argsort(offset_score, axis=1)[:, :P_DEV].astype(jnp.int32)
    place_score = jax.random.randint(key_list[1], (N_GX, N_GY, P_DEV), 0, 1 << 20) * P_DEV + slot_ids
    arrival_place = jnp.argsort(place_score, axis=2).astype(jnp.int32)
    counts = jax.random.randint(key_list[2], (N_GX, N_GY), 0, RMOST + 1)
    busiest = jax.random.randint(key_list[3], (N_GX, 1), 0, N_GY)
    counts = jnp.where(device_ids[None, :] == busiest, RMOST, counts)
    refine_score = jax.random.randint(key_list[4], (N_GX, N_GY, P_DEV), 0, 1 << 20) * P_DEV + slot_ids
    refine_rank = jnp.argsort(jnp.argsort(refine_score, axis=2), axis=2).astype(jnp.int32)
    refined = (refine_rank < counts[:, :, None]).astype(jnp.int32)
    dest_device = (device_ids[None, :, None] + offsets[:, None, :]) % N_GY
    position = arrival_place[row_ids, dest_device, slot_ids[None, None, :]]
    landed_refined = refined[row_ids, dest_device, position]
    old_dest = jnp.where(landed_refined > 0, -1, dest_device * P_DEV + position).astype(jnp.int32)
    owner_row = jax.random.randint(key_list[5], (N_GX, N_GY, 1), 0, N_GX)
    within = jax.random.randint(key_list[6], (N_GX, N_GY, P_DEV), 0, C_DEV * 4)
    parent = (owner_row * (C_DEV * 4) + within).astype(jnp.int32)
    return (old_dest.reshape(N_GX, columns), refined.reshape(N_GX, columns), parent.reshape(N_GX, columns))


def draw_old_dest(key, part):
    return plan_tables(key)[0]


def draw_refine(key, part):
    return plan_tables(key)[1]


def draw_parent_block(key, part):
    return plan_tables(key)[2]


def draw_old_state(key, part):
    key = jax.random.fold_in(key, 11)
    depth_key, flow_key = jax.random.split(key)
    depth_shape = (N_GX, N_GY * P_DEV, 1, CELLS, CELLS)
    flow_shape = (N_GX, N_GY * P_DEV, 2, CELLS, CELLS)
    depth_field = jnp.exp(jax.random.uniform(depth_key, depth_shape, jnp.float32, -0.69, 0.69))
    flow_field = jax.random.normal(flow_key, flow_shape, jnp.float32)
    return jnp.concatenate([depth_field, flow_field], axis=2)


def draw_coarse_state(key, part):
    key = jax.random.fold_in(key, 23)
    depth_key, flow_key = jax.random.split(key)
    depth_shape = (C_DEV * N_GX, N_GY, 1, CELLS, CELLS)
    flow_shape = (C_DEV * N_GX, N_GY, 2, CELLS, CELLS)
    depth_field = jnp.exp(jax.random.uniform(depth_key, depth_shape, jnp.float32, -0.69, 0.69))
    flow_field = jax.random.normal(flow_key, flow_shape, jnp.float32)
    return jnp.concatenate([depth_field, flow_field], axis=2)


def level_of(rng, shape, cuts, low, high):
    def one(dim, shards_of):
        draws = jax.random.uniform(jax.random.fold_in(jax.random.fold_in(rng, 6), dim), (shards_of,), jnp.float32, low / len(cuts), high / len(cuts))
        return jnp.repeat(jnp.exp(draws), shape[dim] // shards_of).reshape((-1,) + (1,) * (len(shape) - dim - 1))

    level = one(*cuts[0])
    for cut in cuts[1:]:
        level = level * one(*cut)
    return level


def bell_draw(key, dims, deviation, reach, shards=(), held_as=jnp.bfloat16):
    drawn = jax.random.normal(key, dims, jnp.float32) * deviation
    if len(shards) > 0:
        drawn = level_of(key, dims, shards, -0.22, 0.18) * drawn
    return jnp.clip(drawn, min=-reach, max=reach).astype(held_as)


def setup_inputs(seed: int = 0) -> dict:
    keys = jax.random.split(jax.random.key(seed), 7)
    return {
        "old_state": draw_old_state(jax.random.fold_in(keys[6], 71), 0),
        "old_dest": draw_old_dest(jax.random.fold_in(keys[6], 71), 0),
        "refine": draw_refine(jax.random.fold_in(keys[6], 71), 0),
        "parent_block": draw_parent_block(jax.random.fold_in(keys[6], 71), 0),
        "coarse_state": draw_coarse_state(jax.random.fold_in(keys[6], 71), 0),
        "force": bell_draw(keys[5], (2, NX, NY), 1.0, 6.0, ((1, 8), (2, 16)), jnp.float32),
    }


omega_relax = 0.8
time_step = 0.5
highest = lax.Precision.HIGHEST


def spread_matrix(cell_count, quarter):
    half_cells = cell_count // 2
    fine_row = jnp.arange(cell_count, dtype=jnp.int32)[:, None]
    coarse_col = jnp.arange(cell_count, dtype=jnp.int32)[None, :]
    middle = fine_row // 2
    beside = jnp.where(fine_row % 2 == 0, middle - 1, middle + 1)
    beside = jnp.clip(beside, 0, half_cells - 1)
    offset_base = quarter * half_cells
    near_part = (coarse_col == offset_base + middle).astype(jnp.float32)
    far_part = (coarse_col == offset_base + beside).astype(jnp.float32)
    return 0.75 * near_part + 0.25 * far_part


def refine_patches(chosen, parent_code):
    first_map = spread_matrix(CELLS, 0)
    second_map = spread_matrix(CELLS, 1)
    quadrant = parent_code % 4
    along_rows = jnp.where((quadrant // 2 == 0)[:, None, None], first_map, second_map)
    along_cols = jnp.where((quadrant % 2 == 0)[:, None, None], first_map, second_map)
    rows_done = jnp.einsum('pia,pkab->pkib', along_rows, chosen, precision=highest)
    return jnp.einsum('pkib,pjb->pkij', rows_done, along_cols, precision=highest)


def face_weights(centre, padded):
    def face_weight(neighbour):
        face_mean = (centre + neighbour) * 0.5
        return face_mean * face_mean * face_mean / 3.0
    face_north = face_weight(padded[:-2, 1:-1])
    face_south = face_weight(padded[2:, 1:-1])
    face_west = face_weight(padded[1:-1, :-2])
    face_east = face_weight(padded[1:-1, 2:])
    return face_north, face_south, face_west, face_east


def relax(velocity, padded, depth_field, face_set, diagonal, right_side):
    face_north, face_south, face_west, face_east = face_set
    applied = depth_field * velocity
    applied = applied + face_north * (velocity - padded[:, :-2, 1:-1])
    applied = applied + face_south * (velocity - padded[:, 2:, 1:-1])
    applied = applied + face_west * (velocity - padded[:, 1:-1, :-2])
    applied = applied + face_east * (velocity - padded[:, 1:-1, 2:])
    return velocity + omega_relax * (right_side - applied) / diagonal


def reference(old_state, old_dest, refine, parent_block, coarse_state, force):
    column_total = old_dest.shape[1]
    row_index = jnp.broadcast_to(jnp.arange(N_GX, dtype=jnp.int32)[:, None], old_dest.shape)
    target = jnp.where(old_dest >= 0, old_dest, column_total).astype(jnp.int32)
    kept_data = jnp.zeros(old_state.shape, jnp.float32).at[row_index, target].set(old_state, mode='drop')
    column_owner = jnp.arange(column_total, dtype=jnp.int32) // P_DEV

    def per_row(packed):
        kept_row, refine_row, parent_row = packed
        chosen = coarse_state[(parent_row // 4).astype(jnp.int32), column_owner]
        refined_data = refine_patches(chosen, parent_row)
        return jnp.where((refine_row > 0)[:, None, None, None], refined_data, kept_row)

    patches = lax.map(per_row, (kept_data, refine, parent_block))
    new_grid = patches.transpose(2, 0, 3, 1, 4).reshape(FIELDS, N_GX * CELLS, column_total * CELLS)
    depth_field = new_grid[0]
    right_side = new_grid[1:] + time_step * force
    face_set = face_weights(depth_field, jnp.pad(depth_field, 1))
    diagonal = depth_field + face_set[0] + face_set[1] + face_set[2] + face_set[3]
    velocity = omega_relax * right_side / diagonal
    for repeat_index in range(SWEEPS - 1):
        padded = jnp.pad(velocity, ((0, 0), (1, 1), (1, 1)))
        velocity = relax(velocity, padded, depth_field, face_set, diagonal, right_side)
    return depth_field, velocity
```

```python
import functools

import jax
import jax.numpy as jnp
from jax import lax
from jax.experimental import pallas as pl
from jax.experimental.pallas import tpu as pltpu
from jax.sharding import PartitionSpec as P

CELLS = 128
FIELDS = 3
SWEEPS = 6
SLOTS = 8
PEERS = 16
HALO = 8
WIDTH = SLOTS * CELLS
EXT_ROWS = CELLS + 2 * HALO
EXT_COLS = WIDTH + CELLS
OMEGA = 0.8
TIME_STEP = 0.5

VMEM_LIMIT = 40 * 1024 * 1024
in_vmem = pl.BlockSpec(memory_space=pltpu.VMEM)
in_smem = pl.BlockSpec(memory_space=pltpu.SMEM)
in_any = pl.BlockSpec(memory_space=pl.ANY)


def params():
    return pltpu.CompilerParams(vmem_limit_bytes=VMEM_LIMIT)


def stage_kernel(dest, old, out, sems):
    def copy(slot, peer):
        return pltpu.make_async_copy(old.at[slot], out.at[peer], sems.at[slot])

    for slot in range(SLOTS):
        target = dest[slot]

        @pl.when(target >= 0)
        def _(slot=slot, target=target):
            copy(slot, target // SLOTS).start()

    for slot in range(SLOTS):
        target = dest[slot]

        @pl.when(target >= 0)
        def _(slot=slot, target=target):
            copy(slot, target // SLOTS).wait()


def stage(dest, old):
    return pl.pallas_call(
        stage_kernel,
        out_shape=jax.ShapeDtypeStruct((PEERS, FIELDS, CELLS, CELLS), jnp.float32),
        in_specs=[in_smem, in_any],
        out_specs=in_any,
        scratch_shapes=[pltpu.SemaphoreType.DMA((SLOTS,))],
        compiler_params=params(),
        name="stage_outgoing",
    )(dest, old)


def spread(quarter, fine_axis):
    fine = lax.broadcasted_iota(jnp.int32, (CELLS, CELLS), fine_axis)
    coarse = lax.broadcasted_iota(jnp.int32, (CELLS, CELLS), 1 - fine_axis)
    half = CELLS // 2
    middle = lax.shift_right_logical(fine, 1)
    beside = jnp.where((fine & 1) == 0, middle - 1, middle + 1)
    beside = jnp.clip(beside, 0, half - 1)
    base = quarter * half
    near = jnp.where(coarse == base + middle, 0.75, 0.0)
    far = jnp.where(coarse == base + beside, 0.25, 0.0)
    return (near + far).astype(jnp.bfloat16)


def split_two(value):
    high = value.astype(jnp.bfloat16)
    low = (value - high.astype(jnp.float32)).astype(jnp.bfloat16)
    return high, low


def dot(a, b):
    return jnp.dot(a, b, preferred_element_type=jnp.float32)


def assemble_kernel(
    source, refine, code, arrived, pieces, force, depth, rhs, left, right, rows, force_v, sems, force_sem
):
    force_copy = pltpu.make_async_copy(force, force_v, force_sem)
    force_copy.start()

    def copies(origin, index, slot):
        cols = pl.ds(slot * CELLS, CELLS)
        return (
            pltpu.make_async_copy(origin.at[index, 0], depth.at[:, cols], sems.at[slot, 0]),
            pltpu.make_async_copy(origin.at[index, 1], rhs.at[0, :, cols], sems.at[slot, 1]),
            pltpu.make_async_copy(origin.at[index, 2], rhs.at[1, :, cols], sems.at[slot, 2]),
        )

    for slot in range(SLOTS):

        @pl.when(refine[slot] > 0)
        def _(slot=slot):
            for copy in copies(pieces, code[slot] // 4, slot):
                copy.start()

        @pl.when(refine[slot] <= 0)
        def _(slot=slot):
            for copy in copies(arrived, source[slot], slot):
                copy.start()

    force_copy.wait()
    for slot in range(SLOTS):
        for copy in copies(arrived, 0, slot):
            copy.wait()
        cols = slice(slot * CELLS, (slot + 1) * CELLS)

        @pl.when(refine[slot] > 0)
        def _(slot=slot, cols=cols):
            quadrant = code[slot] % 4
            along_rows = spread(quadrant // 2, 0)
            along_cols = spread(quadrant % 2, 1)
            for field in range(FIELDS):
                place = depth if field == 0 else rhs.at[field - 1]
                high, low = split_two(place[:, cols])
                done = dot(along_rows, high) + dot(along_rows, low)
                high, low = split_two(done)
                place[:, cols] = dot(high, along_cols) + dot(low, along_cols)

        for field in range(2):
            rhs[field, :, cols] = rhs[field, :, cols] + TIME_STEP * force_v[field, :, cols]

    for field in range(FIELDS):
        place = depth if field == 0 else rhs.at[field - 1]
        left[field] = place[:, :CELLS].T[:HALO]
        right[field] = place[:, WIDTH - CELLS :].T[CELLS - HALO :]
        rows[0, field] = place[:HALO, :]
        rows[1, field] = place[CELLS - HALO :, :]


def assemble(source, refine, code, arrived, pieces, force):
    f32 = jnp.float32
    return pl.pallas_call(
        assemble_kernel,
        out_shape=(
            jax.ShapeDtypeStruct((CELLS, WIDTH), f32),
            jax.ShapeDtypeStruct((2, CELLS, WIDTH), f32),
            jax.ShapeDtypeStruct((FIELDS, HALO, CELLS), f32),
            jax.ShapeDtypeStruct((FIELDS, HALO, CELLS), f32),
            jax.ShapeDtypeStruct((2, FIELDS, HALO, WIDTH), f32),
        ),
        in_specs=[in_smem] * 3 + [in_any] * 3,
        out_specs=[in_vmem] * 5,
        scratch_shapes=[
            pltpu.VMEM((2, CELLS, WIDTH), f32),
            pltpu.SemaphoreType.DMA((SLOTS, FIELDS)),
            pltpu.SemaphoreType.DMA,
        ],
        compiler_params=params(),
        name="assemble_patches",
    )(source, refine, code, arrived, pieces, force)


def edge_kernel(rows, from_left, from_right, top, bottom, side):
    blank = jnp.zeros((CELLS - 2 * HALO, CELLS), jnp.float32)
    for field in range(FIELDS):
        tile = jnp.concatenate([from_right[field], blank, from_left[field]], axis=0).T
        side[field] = tile
        top[field, :, :WIDTH] = rows[0, field]
        top[field, :, WIDTH:] = tile[:HALO]
        bottom[field, :, :WIDTH] = rows[1, field]
        bottom[field, :, WIDTH:] = tile[CELLS - HALO :]


def edges(rows, from_left, from_right):
    f32 = jnp.float32
    return pl.pallas_call(
        edge_kernel,
        out_shape=(
            jax.ShapeDtypeStruct((FIELDS, HALO, EXT_COLS), f32),
            jax.ShapeDtypeStruct((FIELDS, HALO, EXT_COLS), f32),
            jax.ShapeDtypeStruct((FIELDS, CELLS, CELLS), f32),
        ),
        in_specs=[in_vmem] * 3,
        out_specs=[in_vmem] * 3,
        compiler_params=params(),
        name="edge_rows",
    )(rows, from_left, from_right)


TILES = EXT_ROWS // 8


def sweep_kernel(depth, rhs, side, above, below, out, high, right, velo, north, south, west, east):
    def gather(place, field, own):
        place[:HALO] = above[field]
        place[HALO + CELLS :] = below[field]
        place[HALO : HALO + CELLS, :WIDTH] = own
        place[HALO : HALO + CELLS, WIDTH:] = side[field]

    gather(high, 0, depth[...])
    gather(right.at[0], 1, rhs[0])
    gather(right.at[1], 2, rhs[1])

    row = lax.broadcasted_iota(jnp.int32, (8, EXT_COLS), 0)

    def tile(place, t):
        return place[pl.ds(min(max(t, 0), TILES - 1) * 8, 8), :]

    def around(place, t):
        here, before, after = tile(place, t), tile(place, t - 1), tile(place, t + 1)
        up = jnp.where(row == 0, pltpu.roll(before, 1, 0), pltpu.roll(here, 1, 0))
        down = jnp.where(row == 7, pltpu.roll(after, 7, 0), pltpu.roll(here, 7, 0))
        return here, up, down, pltpu.roll(here, 1, 1), pltpu.roll(here, EXT_COLS - 1, 1)

    def weight(a, b):
        mean = (a + b) * 0.5
        return mean * mean * mean * (1.0 / 3.0)

    for t in range(TILES):
        at = slice(t * 8, t * 8 + 8)
        here, *others = around(high, t)
        faces = [weight(here, other) for other in others]
        diagonal = here + faces[0] + faces[1] + faces[2] + faces[3]
        inside = here > 0.0
        scale = jnp.where(inside, OMEGA / jnp.where(inside, diagonal, 1.0), 0.0)
        for place, face in zip((north, south, west, east), faces):
            place[at, :] = face * scale
        for field in range(2):
            start = right[field, at, :] * scale
            right[field, at, :] = start
            velo[0, field, at, :] = start

    def step(s, _):
        now = s % 2
        for t in range(TILES):
            at = slice(t * 8, t * 8 + 8)
            weights = [place[at, :] for place in (north, south, west, east)]
            for field in range(2):
                here, *others = around(velo.at[now, field], t)
                total = right[field, at, :] + (1.0 - OMEGA) * here
                for w, other in zip(weights, others):
                    total = total + w * other
                velo[1 - now, field, at, :] = total
        return 0

    lax.fori_loop(0, SWEEPS - 1, step, 0)
    last = (SWEEPS - 1) % 2
    out[...] = velo[last, :, HALO : HALO + CELLS, :WIDTH]


def sweeps(depth, rhs, side, above, below):
    f32 = jnp.float32
    ext = (EXT_ROWS, EXT_COLS)
    return pl.pallas_call(
        sweep_kernel,
        out_shape=jax.ShapeDtypeStruct((2, CELLS, WIDTH), f32),
        in_specs=[in_vmem] * 5,
        out_specs=in_vmem,
        scratch_shapes=[
            pltpu.VMEM(ext, f32),
            pltpu.VMEM((2,) + ext, f32),
            pltpu.VMEM((2, 2) + ext, f32),
        ]
        + [pltpu.VMEM(ext, f32)] * 4,
        compiler_params=params(),
        name="jacobi_sweeps",
    )(depth, rhs, side, above, below)


def moved(value, axis, step):
    count = lax.axis_size(axis)
    pairs = [(i, i + step) for i in range(count) if 0 <= i + step < count]
    return lax.ppermute(value, axis, pairs)


def body(old_state, old_dest, refine, parent_block, coarse_state, force):
    dest = old_dest[0]
    table = lax.all_gather(dest, "gy", axis=0)
    pieces = lax.all_gather(coarse_state[:, 0], "gx", axis=0, tiled=True)
    outgoing = stage(dest, old_state[0])
    arrived = lax.all_to_all(outgoing, "gy", split_axis=0, concat_axis=0, tiled=True)
    place = table - lax.axis_index("gy") * SLOTS
    hit = place[None] == jnp.arange(SLOTS, dtype=jnp.int32)[:, None, None]
    peer = jnp.arange(PEERS, dtype=jnp.int32)[None, :, None]
    source = jnp.max(jnp.where(hit, peer, 0), axis=(1, 2))
    depth, rhs, left, right, rows = assemble(
        source, refine[0], parent_block[0], arrived, pieces, force
    )
    from_left = moved(right, "gy", 1)
    from_right = moved(left, "gy", -1)
    top, bottom, side = edges(rows, from_left, from_right)
    above = moved(bottom, "gx", 1)
    below = moved(top, "gx", -1)
    velocity = sweeps(depth, rhs, side, above, below)
    return depth, velocity


def solution(mesh):
    return jax.shard_map(
        body,
        mesh=mesh,
        in_specs=(
            P("gx", "gy", None, None, None),
            P("gx", "gy"),
            P("gx", "gy"),
            P("gx", "gy"),
            P("gx", "gy", None, None, None),
            P(None, "gx", "gy"),
        ),
        out_specs=(P("gx", "gy"), P(None, "gx", "gy")),
        check_vma=False,
    )
```

```python
import functools

import jax
import jax.numpy as jnp
from jax import lax
from jax.experimental import pallas as pl
from jax.experimental.pallas import tpu as pltpu
from jax.sharding import PartitionSpec as P

CELLS = 128
FIELDS = 3
SWEEPS = 6
SLOTS = 8
PEERS = 16
OWNERS = 8
HALO = 8
WIDTH = SLOTS * CELLS
PATCH_ROWS = FIELDS * CELLS
CHUNK_ROWS = PATCH_ROWS + HALO
EXT_ROWS = CELLS + 2 * HALO
TILES = EXT_ROWS // 8
BLOCKS = SLOTS + 1
EXT_COLS = BLOCKS * CELLS
OMEGA = 0.8
TIME_STEP = 0.5

MIB = 1024 * 1024
in_vmem = pl.BlockSpec(memory_space=pltpu.VMEM)
in_smem = pl.BlockSpec(memory_space=pltpu.SMEM)
in_any = pl.BlockSpec(memory_space=pl.ANY)


def params(mib):
    return pltpu.CompilerParams(vmem_limit_bytes=mib * MIB)


def stage_kernel(dest, old, out, patch_v, note_v, in_sems, out_sems, note_sem):
    for slot in range(SLOTS):
        pltpu.make_async_copy(old.at[slot], patch_v.at[slot], in_sems.at[slot]).start()
    note_v[...] = jnp.full(note_v.shape, -1.0, jnp.float32)
    for slot in range(SLOTS):
        target = dest[slot]

        @pl.when(target >= 0)
        def _(target=target):
            where = lax.convert_element_type(target & (SLOTS - 1), jnp.float32)
            note_v[target >> 3] = jnp.full((HALO, CELLS), where, jnp.float32)

    notes = pltpu.make_async_copy(note_v, out.at[:, pl.ds(PATCH_ROWS, HALO)], note_sem)
    notes.start()

    def send(slot):
        rows = out.at[dest[slot] >> 3, pl.ds(0, PATCH_ROWS)]
        return pltpu.make_async_copy(patch_v.at[slot], rows, out_sems.at[slot])

    for slot in range(SLOTS):
        pltpu.make_async_copy(old.at[slot], patch_v.at[slot], in_sems.at[slot]).wait()

        @pl.when(dest[slot] >= 0)
        def _(slot=slot):
            send(slot).start()

    for slot in range(SLOTS):

        @pl.when(dest[slot] >= 0)
        def _(slot=slot):
            send(slot).wait()

    notes.wait()


def stage(dest, old):
    return pl.pallas_call(
        stage_kernel,
        out_shape=jax.ShapeDtypeStruct((PEERS, CHUNK_ROWS, CELLS), jnp.float32),
        in_specs=[in_smem, in_any],
        out_specs=in_any,
        scratch_shapes=[
            pltpu.VMEM((SLOTS, PATCH_ROWS, CELLS), jnp.float32),
            pltpu.VMEM((PEERS, HALO, CELLS), jnp.float32),
            pltpu.SemaphoreType.DMA((SLOTS,)),
            pltpu.SemaphoreType.DMA((SLOTS,)),
            pltpu.SemaphoreType.DMA,
        ],
        compiler_params=params(60),
        name="stage_outgoing",
    )(dest, old)


def spread(quarter, fine_axis):
    fine = lax.broadcasted_iota(jnp.int32, (CELLS, CELLS), fine_axis)
    coarse = lax.broadcasted_iota(jnp.int32, (CELLS, CELLS), 1 - fine_axis)
    half = CELLS // 2
    middle = lax.shift_right_logical(fine, 1)
    beside = jnp.where((fine & 1) == 0, middle - 1, middle + 1)
    beside = jnp.clip(beside, 0, half - 1)
    base = quarter * half
    near = jnp.where(coarse == base + middle, 0.75, 0.0)
    far = jnp.where(coarse == base + beside, 0.25, 0.0)
    return (near + far).astype(jnp.bfloat16)


def split_two(value):
    high = value.astype(jnp.bfloat16)
    low = (value - high.astype(jnp.float32)).astype(jnp.bfloat16)
    return high, low


def dot(a, b):
    return jnp.dot(a, b, preferred_element_type=jnp.float32)


def assemble_kernel(refine, code, owner, arrived, force, *refs):
    pieces, refs = refs[:OWNERS], refs[OWNERS:]
    depth, state, left, right, rows, note_v, note_i, force_v, sems, note_sem, force_sem, depth_sem = refs
    notes = pltpu.make_async_copy(arrived.at[:, pl.ds(PATCH_ROWS, HALO)], note_v, note_sem)
    notes.start()

    def force_copy(slot):
        cols = pl.ds(slot * CELLS, CELLS)
        return pltpu.make_async_copy(force.at[:, :, cols], force_v.at[slot], force_sem.at[slot])

    for slot in range(SLOTS):
        force_copy(slot).start()

    def place(origin, slot):
        return pltpu.make_async_copy(origin, state.at[slot], sems.at[slot])

    for number, piece in enumerate(pieces):

        @pl.when(owner[0] == number)
        def _(piece=piece):
            for slot in range(SLOTS):

                @pl.when(refine[slot] > 0)
                def _(slot=slot):
                    place(piece.at[(code[slot] >> 2) & 1], slot).start()

    notes.wait()
    note_i[...] = note_v[:, 0, :].astype(jnp.int32)
    for peer in range(PEERS):
        slot = note_i[peer, 0]

        @pl.when(slot >= 0)
        def _(slot=slot, peer=peer):
            place(arrived.at[peer, pl.ds(0, PATCH_ROWS)], slot).start()

    def depth_copy(slot):
        cols = pl.ds(slot * CELLS, CELLS)
        source = state.at[slot, pl.ds(0, CELLS)]
        return pltpu.make_async_copy(source, depth.at[:, cols], depth_sem.at[slot])

    for slot in range(SLOTS):
        place(arrived.at[0, pl.ds(0, PATCH_ROWS)], slot).wait()

        @pl.when(refine[slot] > 0)
        def _(slot=slot):
            quadrant = code[slot] & 3
            along_rows = spread(quadrant >> 1, 0)
            along_cols = spread(quadrant & 1, 1)
            for field in range(FIELDS):
                at = slice(field * CELLS, (field + 1) * CELLS)
                high, low = split_two(state[slot, at])
                done = dot(along_rows, high) + dot(along_rows, low)
                high, low = split_two(done)
                state[slot, at] = dot(high, along_cols) + dot(low, along_cols)

        depth_copy(slot).start()
        force_copy(slot).wait()
        for field in range(2):
            at = slice((field + 1) * CELLS, (field + 2) * CELLS)
            state[slot, at] = state[slot, at] + TIME_STEP * force_v[slot, field]
        for field in range(FIELDS):
            low = field * CELLS
            rows[0, field, slot] = state[slot, low : low + HALO]
            rows[1, field, slot] = state[slot, low + CELLS - HALO : low + CELLS]

    for field in range(FIELDS):
        at = slice(field * CELLS, (field + 1) * CELLS)
        left[field] = state[0, at].T[:HALO]
        right[field] = state[SLOTS - 1, at].T[CELLS - HALO :]
    for slot in range(SLOTS):
        depth_copy(slot).wait()


def assemble(refine, code, owner, arrived, force, pieces):
    f32 = jnp.float32
    return pl.pallas_call(
        assemble_kernel,
        out_shape=(
            jax.ShapeDtypeStruct((CELLS, WIDTH), f32),
            jax.ShapeDtypeStruct((SLOTS, PATCH_ROWS, CELLS), f32),
            jax.ShapeDtypeStruct((FIELDS, HALO, CELLS), f32),
            jax.ShapeDtypeStruct((FIELDS, HALO, CELLS), f32),
            jax.ShapeDtypeStruct((2, FIELDS, SLOTS, HALO, CELLS), f32),
        ),
        in_specs=[in_smem] * 3 + [in_any] * (2 + OWNERS),
        out_specs=[in_any] + [in_vmem] * 4,
        scratch_shapes=[
            pltpu.VMEM((PEERS, HALO, CELLS), f32),
            pltpu.VMEM((PEERS, CELLS), jnp.int32),
            pltpu.VMEM((SLOTS, 2, CELLS, CELLS), f32),
            pltpu.SemaphoreType.DMA((SLOTS,)),
            pltpu.SemaphoreType.DMA,
            pltpu.SemaphoreType.DMA((SLOTS,)),
            pltpu.SemaphoreType.DMA((SLOTS,)),
        ],
        compiler_params=params(40),
        name="assemble_patches",
    )(refine, code, owner, arrived, force, *pieces)


def edge_kernel(rows, from_left, from_right, top, bottom, side):
    blank = jnp.zeros((CELLS - 2 * HALO, CELLS), jnp.float32)
    for field in range(FIELDS):
        tile = jnp.concatenate([from_right[field], blank, from_left[field]], axis=0).T
        side[field] = tile
        top[field, :SLOTS] = rows[0, field]
        top[field, SLOTS] = tile[:HALO]
        bottom[field, :SLOTS] = rows[1, field]
        bottom[field, SLOTS] = tile[CELLS - HALO :]


def edges(rows, from_left, from_right):
    f32 = jnp.float32
    return pl.pallas_call(
        edge_kernel,
        out_shape=(
            jax.ShapeDtypeStruct((FIELDS, BLOCKS, HALO, CELLS), f32),
            jax.ShapeDtypeStruct((FIELDS, BLOCKS, HALO, CELLS), f32),
            jax.ShapeDtypeStruct((FIELDS, CELLS, CELLS), f32),
        ),
        in_specs=[in_vmem] * 3,
        out_specs=[in_vmem] * 3,
        compiler_params=params(16),
        name="edge_rows",
    )(rows, from_left, from_right)


def sweep_kernel(state, side, above, below, out, wide, right, velo, faces, out_sems):
    for field in range(FIELDS):
        at = slice(field * CELLS, (field + 1) * CELLS)
        for block in range(BLOCKS):
            wide[field, block, :HALO] = above[field, block]
            wide[field, block, HALO + CELLS :] = below[field, block]
            wide[field, block, HALO : HALO + CELLS] = side[field] if block == SLOTS else state[block, at]

    def rows_of(t):
        return pl.ds(t, 8, stride=TILES)

    def spaced(field, t):
        return jnp.concatenate([wide[field, block, rows_of(t), :] for block in range(BLOCKS)], axis=1)

    def each_tile(load):
        first, last = load(0), load(TILES - 1)
        before, here = pltpu.roll(last, 1, 0), first
        for t in range(TILES):
            after = load(t + 1) if t < TILES - 1 else pltpu.roll(load(0), 7, 0)
            yield t, here, (before, after, pltpu.roll(here, 1, 1), pltpu.roll(here, EXT_COLS - 1, 1))
            before, here = here, after

    def weight(a, b):
        mean = (a + b) * 0.5
        return mean * mean * mean * (1.0 / 3.0)

    for t, here, others in each_tile(lambda t: spaced(0, t)):
        weights = [weight(here, other) for other in others]
        diagonal = here + weights[0] + weights[1] + weights[2] + weights[3]
        inside = here > 0.0
        scale = jnp.where(inside, OMEGA / jnp.where(inside, diagonal, 1.0), 0.0)
        for number, w in enumerate(weights):
            faces[number, t] = w * scale
        for field in range(2):
            start = spaced(field + 1, t) * scale
            right[field, t] = start
            velo[0, field, t] = start

    def relaxed(now, field, t, here, others):
        total = right[field, t] + (1.0 - OMEGA) * here
        for number, other in enumerate(others):
            total = total + faces[number, t] * other
        return total

    def step(s, _):
        now = s & 1
        for field in range(2):
            for t, here, others in each_tile(lambda t: velo[now, field, t]):
                velo[1 - now, field, t] = relaxed(now, field, t, here, others)
        return 0

    lax.fori_loop(0, SWEEPS - 2, step, 0)

    def out_copy(field, block):
        cols = pl.ds(block * CELLS, CELLS)
        source = wide.at[field, block, pl.ds(HALO, CELLS)]
        return pltpu.make_async_copy(source, out.at[field, :, cols], out_sems.at[field, block])

    now = (SWEEPS - 2) % 2
    for field in range(2):
        for t, here, others in each_tile(lambda t: velo[now, field, t]):
            done = relaxed(now, field, t, here, others)
            for block in range(SLOTS):
                wide[field, block, rows_of(t), :] = done[:, block * CELLS : (block + 1) * CELLS]
        for block in range(SLOTS):
            out_copy(field, block).start()
    for field in range(2):
        for block in range(SLOTS):
            out_copy(field, block).wait()


def sweeps(state, side, above, below):
    f32 = jnp.float32
    tiles = (TILES, 8, EXT_COLS)
    return pl.pallas_call(
        sweep_kernel,
        out_shape=jax.ShapeDtypeStruct((2, CELLS, WIDTH), f32),
        in_specs=[in_vmem] * 4,
        out_specs=in_any,
        scratch_shapes=[
            pltpu.VMEM((FIELDS, BLOCKS, EXT_ROWS, CELLS), f32),
            pltpu.VMEM((2,) + tiles, f32),
            pltpu.VMEM((2, 2) + tiles, f32),
            pltpu.VMEM((4,) + tiles, f32),
            pltpu.SemaphoreType.DMA((2, SLOTS)),
        ],
        compiler_params=params(40),
        name="jacobi_sweeps",
    )(state, side, above, below)


def moved(value, axis, step):
    count = lax.axis_size(axis)
    pairs = [(i, i + step) for i in range(count) if 0 <= i + step < count]
    return lax.ppermute(value, axis, pairs)


def around_ring(value, axis, step):
    count = lax.axis_size(axis)
    return lax.ppermute(value, axis, [(i, (i + step) % count) for i in range(count)])


def swapped(value, axis, bit):
    count = lax.axis_size(axis)
    return lax.ppermute(value, axis, [(i, i ^ bit) for i in range(count)])


def column_pieces(coarse):
    own = [
        coarse,
        around_ring(coarse, "gx", -2),
        around_ring(coarse, "gx", 4),
        around_ring(coarse, "gx", 2),
    ]
    return own + [swapped(piece, "gx", 1) for piece in own]


def body(old_state, old_dest, refine, parent_block, coarse_state, force):
    gx = lax.axis_index("gx")
    outgoing = stage(old_dest[0], old_state.reshape(SLOTS, PATCH_ROWS, CELLS))
    arrived = lax.all_to_all(outgoing, "gy", split_axis=0, concat_axis=0, tiled=True)
    pieces = column_pieces(coarse_state.reshape(2, PATCH_ROWS, CELLS))
    holder = parent_block[0, :1] >> 3
    owner = (((holder >> 1) - (gx >> 1)) & 3) + 4 * ((holder ^ gx) & 1)
    depth, state, left, right, rows = assemble(
        refine[0], parent_block[0], owner, arrived, force, pieces
    )
    from_left = moved(right, "gy", 1)
    from_right = moved(left, "gy", -1)
    top, bottom, side = edges(rows, from_left, from_right)
    above = moved(bottom, "gx", 1)
    below = moved(top, "gx", -1)
    velocity = sweeps(state, side, above, below)
    return depth, velocity


def solution(mesh):
    return jax.shard_map(
        body,
        mesh=mesh,
        in_specs=(
            P("gx", "gy", None, None, None),
            P("gx", "gy"),
            P("gx", "gy"),
            P("gx", "gy"),
            P("gx", "gy", None, None, None),
            P(None, "gx", "gy"),
        ),
        out_specs=(P("gx", "gy"), P(None, "gx", "gy")),
        check_vma=False,
    )
```

```python
import functools

import jax
import jax.numpy as jnp
from jax import lax
from jax.experimental import pallas as pl
from jax.experimental.pallas import tpu as pltpu
from jax.sharding import PartitionSpec as P

CELLS = 128
FIELDS = 3
SWEEPS = 6
SLOTS = 8
PEERS = 16
OWNERS = 8
REFINED = 2
HALO = 8
WIDTH = SLOTS * CELLS
PATCH_ROWS = FIELDS * CELLS
CHUNK_ROWS = PATCH_ROWS + HALO
EXT_ROWS = CELLS + 2 * HALO
TILES = EXT_ROWS // 8
BLOCKS = SLOTS + 1
EXT_COLS = BLOCKS * CELLS
OMEGA = 0.8
TIME_STEP = 0.5

MIB = 1024 * 1024
in_vmem = pl.BlockSpec(memory_space=pltpu.VMEM)
in_smem = pl.BlockSpec(memory_space=pltpu.SMEM)
in_hbm = pl.BlockSpec(memory_space=pltpu.HBM)
in_any = pl.BlockSpec(memory_space=pl.ANY)


def params(mib):
    return pltpu.CompilerParams(vmem_limit_bytes=mib * MIB)


def stage_kernel(dest, old, out, patch_v, note_v, in_sems, out_sems, note_sem):
    for slot in range(SLOTS):
        pltpu.make_async_copy(old.at[slot], patch_v.at[slot], in_sems.at[slot]).start()
    note_v[...] = jnp.full(note_v.shape, -1.0, jnp.float32)
    for slot in range(SLOTS):
        target = dest[slot]

        @pl.when(target >= 0)
        def _(target=target):
            where = lax.convert_element_type(target & (SLOTS - 1), jnp.float32)
            note_v[target >> 3] = jnp.full((HALO, CELLS), where, jnp.float32)

    notes = pltpu.make_async_copy(note_v, out.at[:, pl.ds(PATCH_ROWS, HALO)], note_sem)
    notes.start()

    def send(slot):
        rows = out.at[dest[slot] >> 3, pl.ds(0, PATCH_ROWS)]
        return pltpu.make_async_copy(patch_v.at[slot], rows, out_sems.at[slot])

    for slot in range(SLOTS):
        pltpu.make_async_copy(old.at[slot], patch_v.at[slot], in_sems.at[slot]).wait()

        @pl.when(dest[slot] >= 0)
        def _(slot=slot):
            send(slot).start()

    for slot in range(SLOTS):

        @pl.when(dest[slot] >= 0)
        def _(slot=slot):
            send(slot).wait()

    notes.wait()


def stage(dest, old):
    return pl.pallas_call(
        stage_kernel,
        out_shape=jax.ShapeDtypeStruct((PEERS, CHUNK_ROWS, CELLS), jnp.float32),
        in_specs=[in_smem, in_hbm],
        out_specs=in_any,
        scratch_shapes=[
            pltpu.VMEM((SLOTS, PATCH_ROWS, CELLS), jnp.float32),
            pltpu.VMEM((PEERS, HALO, CELLS), jnp.float32),
            pltpu.SemaphoreType.DMA((SLOTS,)),
            pltpu.SemaphoreType.DMA((SLOTS,)),
            pltpu.SemaphoreType.DMA,
        ],
        compiler_params=params(60),
        name="stage_outgoing",
    )(dest, old)


KEPT = 4
COLS_AT = 2 * PATCH_ROWS
ROWS_AT = COLS_AT + 4 * CELLS


def keep_kernel(force, coarse, out, kept_v, sems, out_sem):
    copies = [(coarse.at[0], 0, PATCH_ROWS), (coarse.at[1], PATCH_ROWS, PATCH_ROWS)]
    for field in range(2):
        for edge in range(2):
            number = field * 2 + edge
            cols = pl.ds(edge * (WIDTH - CELLS), CELLS)
            copies.append((force.at[field, :, cols], COLS_AT + number * CELLS, CELLS))
            for slot in range(SLOTS):
                part = force.at[field, pl.ds(edge * (CELLS - HALO), HALO), pl.ds(slot * CELLS, CELLS)]
                copies.append((part, ROWS_AT + (number * SLOTS + slot) * HALO, HALO))
    copies = [
        pltpu.make_async_copy(part, kept_v.at[pl.ds(first, size)], sems.at[number])
        for number, (part, first, size) in enumerate(copies)
    ]
    for copy in copies:
        copy.start()
    for copy in copies:
        copy.wait()
    last = pltpu.make_async_copy(kept_v, out, out_sem)
    last.start()
    last.wait()


def keep(force, coarse):
    shape = (KEPT * PATCH_ROWS, CELLS)
    return pl.pallas_call(
        keep_kernel,
        out_shape=jax.ShapeDtypeStruct(shape, jnp.float32),
        in_specs=[in_any] * 2,
        out_specs=in_any,
        scratch_shapes=[
            pltpu.VMEM(shape, jnp.float32),
            pltpu.SemaphoreType.DMA((6 + 4 * SLOTS,)),
            pltpu.SemaphoreType.DMA,
        ],
        compiler_params=params(24),
        cost_estimate=pl.CostEstimate(flops=1 << 18, bytes_accessed=3 << 20, transcendentals=0),
        name="keep_own",
    )(force, coarse)


def spread(quarter, fine_axis):
    fine = lax.broadcasted_iota(jnp.int32, (CELLS, CELLS), fine_axis)
    coarse = lax.broadcasted_iota(jnp.int32, (CELLS, CELLS), 1 - fine_axis)
    half = CELLS // 2
    middle = lax.shift_right_logical(fine, 1)
    beside = jnp.where((fine & 1) == 0, middle - 1, middle + 1)
    beside = jnp.clip(beside, 0, half - 1)
    base = quarter * half
    near = jnp.where(coarse == base + middle, 0.75, 0.0)
    far = jnp.where(coarse == base + beside, 0.25, 0.0)
    return (near + far).astype(jnp.bfloat16)


def split_two(value):
    high = value.astype(jnp.bfloat16)
    low = (value - high.astype(jnp.float32)).astype(jnp.bfloat16)
    return high, low


def dot(a, b):
    return jnp.dot(a, b, preferred_element_type=jnp.float32)


def outline_kernel(refine, code, owner, arrived, *refs):
    pieces, refs = refs[:OWNERS], refs[OWNERS:]
    source, fresh, left, right, rows, parent_v, note_i, force_v, picks, sems, force_sem = refs
    force_copy = pltpu.make_async_copy(pieces[0].at[pl.ds(2, 2)], force_v, force_sem)
    force_copy.start()

    picks[0] = -1
    picks[1] = -1
    count = jnp.int32(0)
    for slot in range(SLOTS):
        here = refine[slot] > 0
        source[slot] = jnp.where(here, PEERS + count, 0)

        @pl.when(here)
        def _(slot=slot, count=count):
            picks[jnp.minimum(count, REFINED - 1)] = slot

        count = count + here.astype(jnp.int32)

    def quarter(piece, number, field):
        slot = picks[number]
        first = pl.multiple_of(field * CELLS + ((code[slot] >> 1) & 1) * (CELLS // 2), CELLS // 2)
        return pltpu.make_async_copy(
            piece.at[(code[slot] >> 2) & 1, pl.ds(first, CELLS // 2)],
            parent_v.at[number, field],
            sems.at[number],
        )

    for place, piece in enumerate(pieces):

        @pl.when(owner[0] == place)
        def _(piece=piece):
            for number in range(REFINED):

                @pl.when(picks[number] >= 0)
                def _(number=number):
                    for field in range(FIELDS):
                        quarter(piece, number, field).start()

    note_i[...] = arrived[:, PATCH_ROWS, :].astype(jnp.int32)
    for peer in range(PEERS):
        slot = note_i[peer, 0]

        @pl.when(slot >= 0)
        def _(slot=slot, peer=peer):
            source[slot] = peer

    def refined(number, _):
        @pl.when(picks[number] >= 0)
        def _():
            for field in range(FIELDS):
                quarter(pieces[0], number, field).wait()
            along_rows = spread(0, 0)[:, : CELLS // 2]
            along_cols = spread(code[picks[number]] & 1, 1)
            for field in range(FIELDS):
                high, low = split_two(parent_v[number, field])
                done = dot(along_rows, high) + dot(along_rows, low)
                high, low = split_two(done)
                at = slice(field * CELLS, (field + 1) * CELLS)
                fresh[number, at] = dot(high, along_cols) + dot(low, along_cols)

        return 0

    lax.fori_loop(0, REFINED, refined, 0)

    def taken(slot, first, size):
        origin = source[slot]
        kept = arrived[jnp.minimum(origin, PEERS - 1), first : first + size]
        new = fresh[jnp.clip(origin - PEERS, 0, REFINED - 1), first : first + size]
        return jnp.where(origin >= PEERS, new, kept)

    def forcing(first, size):
        part, first = divmod(first - COLS_AT, PATCH_ROWS)
        return TIME_STEP * force_v[part, first : first + size]

    force_copy.wait()
    for field in range(FIELDS):
        low = field * CELLS
        first = taken(0, low, CELLS)
        last = taken(SLOTS - 1, low, CELLS)
        if field > 0:
            first = first + forcing(COLS_AT + (2 * field - 2) * CELLS, CELLS)
            last = last + forcing(COLS_AT + (2 * field - 1) * CELLS, CELLS)
        left[field] = first.T[:HALO]
        right[field] = last.T[CELLS - HALO :]
        for slot in range(SLOTS):
            for edge, first in enumerate((low, low + CELLS - HALO)):
                value = taken(slot, first, HALO)
                if field > 0:
                    number = 2 * field - 2 + edge
                    value = value + forcing(ROWS_AT + (number * SLOTS + slot) * HALO, HALO)
                rows[edge, field, slot] = value


def outline(refine, code, owner, arrived, pieces):
    f32 = jnp.float32
    return pl.pallas_call(
        outline_kernel,
        out_shape=(
            jax.ShapeDtypeStruct((SLOTS,), jnp.int32),
            jax.ShapeDtypeStruct((REFINED, PATCH_ROWS, CELLS), f32),
            jax.ShapeDtypeStruct((FIELDS, HALO, CELLS), f32),
            jax.ShapeDtypeStruct((FIELDS, HALO, CELLS), f32),
            jax.ShapeDtypeStruct((2, FIELDS, SLOTS, HALO, CELLS), f32),
        ),
        in_specs=[in_smem] * 3 + [in_vmem] + [in_any] * OWNERS,
        out_specs=[in_smem] + [in_vmem] * 4,
        scratch_shapes=[
            pltpu.VMEM((REFINED, FIELDS, CELLS // 2, CELLS), f32),
            pltpu.VMEM((PEERS, CELLS), jnp.int32),
            pltpu.VMEM((2, PATCH_ROWS, CELLS), f32),
            pltpu.SMEM((REFINED,), jnp.int32),
            pltpu.SemaphoreType.DMA((REFINED,)),
            pltpu.SemaphoreType.DMA,
        ],
        compiler_params=params(40),
        name="block_outline",
    )(refine, code, owner, arrived, *pieces)


def interior_kernel(source, arrived, fresh, force, depth, wide, force_v, force_sems, depth_sems):
    force_copies = [pltpu.make_async_copy(force.at[i], force_v.at[i], force_sems.at[i]) for i in range(2)]
    for copy in force_copies:
        copy.start()

    def depth_copy(slot):
        inner = wide.at[0, slot, pl.ds(HALO, CELLS)]
        cols = pl.ds(slot * CELLS, CELLS)
        return pltpu.make_async_copy(inner, depth.at[:, cols], depth_sems.at[slot])

    for field in range(FIELDS):
        if field > 0:
            force_copies[field - 1].wait()
        for slot in range(SLOTS):
            origin = source[slot]
            at = slice(field * CELLS, (field + 1) * CELLS)
            kept = arrived[jnp.minimum(origin, PEERS - 1), at]
            new = fresh[jnp.clip(origin - PEERS, 0, REFINED - 1), at]
            value = jnp.where(origin >= PEERS, new, kept)
            if field > 0:
                value = value + TIME_STEP * force_v[field - 1, :, slot * CELLS : (slot + 1) * CELLS]
            wide[field, slot, HALO : HALO + CELLS] = value
            if field == 0:
                depth_copy(slot).start()
    for slot in range(SLOTS):
        depth_copy(slot).wait()


def interior(source, arrived, fresh, force):
    f32 = jnp.float32
    return pl.pallas_call(
        interior_kernel,
        out_shape=(
            jax.ShapeDtypeStruct((CELLS, WIDTH), f32),
            jax.ShapeDtypeStruct((FIELDS, SLOTS, EXT_ROWS, CELLS), f32),
        ),
        in_specs=[in_smem] + [in_vmem] * 2 + [in_hbm],
        out_specs=[in_hbm, in_vmem],
        scratch_shapes=[
            pltpu.VMEM((2, CELLS, WIDTH), f32),
            pltpu.SemaphoreType.DMA((2,)),
            pltpu.SemaphoreType.DMA((SLOTS,)),
        ],
        compiler_params=params(24),
        cost_estimate=pl.CostEstimate(flops=1 << 20, bytes_accessed=6 << 20, transcendentals=0),
        name="block_interior",
    )(source, arrived, fresh, force)


def edge_kernel(rows, from_left, from_right, top, bottom, side):
    blank = jnp.zeros((CELLS - 2 * HALO, CELLS), jnp.float32)
    for field in range(FIELDS):
        tile = jnp.concatenate([from_right[field], blank, from_left[field]], axis=0).T
        side[field, :HALO] = tile[:HALO]
        side[field, HALO : HALO + CELLS] = tile
        side[field, HALO + CELLS :] = tile[:HALO]
        for block in range(SLOTS):
            at = slice(block * CELLS, (block + 1) * CELLS)
            top[field, :, at] = rows[0, field, block]
            bottom[field, :, at] = rows[1, field, block]
        top[field, :, WIDTH:] = tile[:HALO]
        bottom[field, :, WIDTH:] = tile[CELLS - HALO :]


def edges(rows, from_left, from_right):
    f32 = jnp.float32
    return pl.pallas_call(
        edge_kernel,
        out_shape=(
            jax.ShapeDtypeStruct((FIELDS, HALO, EXT_COLS), f32),
            jax.ShapeDtypeStruct((FIELDS, HALO, EXT_COLS), f32),
            jax.ShapeDtypeStruct((FIELDS, EXT_ROWS, CELLS), f32),
        ),
        in_specs=[in_vmem] * 3,
        out_specs=[in_vmem] * 3,
        compiler_params=params(16),
        name="edge_rows",
    )(rows, from_left, from_right)


def sweep_kernel(inner, side, above, below, out, done_v, right, velo, faces, out_sems):
    row = lax.broadcasted_iota(jnp.int32, (8, EXT_COLS), 0)

    def rows_of(t):
        return pl.ds(t, 8, stride=TILES)

    def spaced(field, t):
        parts = [inner[field, block, rows_of(t), :] for block in range(SLOTS)]
        value = jnp.concatenate(parts + [side[field, rows_of(t), :]], axis=1)
        if t < HALO:
            value = jnp.where(row == 0, above[field, t : t + 1, :], value)
        if t >= TILES - HALO:
            first = t - (TILES - HALO)
            value = jnp.where(row == 7, below[field, first : first + 1, :], value)
        return value

    def each_tile(load):
        first, last = load(0), load(TILES - 1)
        before, here = pltpu.roll(last, 1, 0), first
        for t in range(TILES):
            after = load(t + 1) if t < TILES - 1 else pltpu.roll(load(0), 7, 0)
            yield t, here, (before, after, pltpu.roll(here, 1, 1), pltpu.roll(here, EXT_COLS - 1, 1))
            before, here = here, after

    def weight(a, b):
        mean = (a + b) * 0.5
        return mean * mean * mean * (1.0 / 3.0)

    for t, here, others in each_tile(lambda t: spaced(0, t)):
        weights = [weight(here, other) for other in others]
        diagonal = here + weights[0] + weights[1] + weights[2] + weights[3]
        inside = here > 0.0
        scale = jnp.where(inside, OMEGA / jnp.where(inside, diagonal, 1.0), 0.0)
        for number, w in enumerate(weights):
            faces[number, t] = w * scale
        for field in range(2):
            start = spaced(field + 1, t) * scale
            right[field, t] = start
            velo[0, field, t] = start

    def relaxed(now, field, t, here, others):
        total = right[field, t] + (1.0 - OMEGA) * here
        for number, other in enumerate(others):
            total = total + faces[number, t] * other
        return total

    def step(s, _):
        now = s & 1
        for field in range(2):
            for t, here, others in each_tile(lambda t: velo[now, field, t]):
                velo[1 - now, field, t] = relaxed(now, field, t, here, others)
        return 0

    lax.fori_loop(0, SWEEPS - 2, step, 0)

    def out_copy(field, block):
        cols = pl.ds(block * CELLS, CELLS)
        source = done_v.at[field, block, pl.ds(HALO, CELLS)]
        return pltpu.make_async_copy(source, out.at[field, :, cols], out_sems.at[field, block])

    now = (SWEEPS - 2) % 2
    for field in range(2):
        for t, here, others in each_tile(lambda t: velo[now, field, t]):
            done = relaxed(now, field, t, here, others)
            for block in range(SLOTS):
                done_v[field, block, rows_of(t), :] = done[:, block * CELLS : (block + 1) * CELLS]
        for block in range(SLOTS):
            out_copy(field, block).start()
    for field in range(2):
        for block in range(SLOTS):
            out_copy(field, block).wait()


def sweeps(inner, side, above, below):
    f32 = jnp.float32
    tiles = (TILES, 8, EXT_COLS)
    return pl.pallas_call(
        sweep_kernel,
        out_shape=jax.ShapeDtypeStruct((2, CELLS, WIDTH), f32),
        in_specs=[in_vmem] * 4,
        out_specs=in_any,
        scratch_shapes=[
            pltpu.VMEM((2, SLOTS, EXT_ROWS, CELLS), f32),
            pltpu.VMEM((2,) + tiles, f32),
            pltpu.VMEM((2, 2) + tiles, f32),
            pltpu.VMEM((4,) + tiles, f32),
            pltpu.SemaphoreType.DMA((2, SLOTS)),
        ],
        compiler_params=params(40),
        name="jacobi_sweeps",
    )(inner, side, above, below)


def moved(value, axis, step):
    count = lax.axis_size(axis)
    pairs = [(i, i + step) for i in range(count) if 0 <= i + step < count]
    return lax.ppermute(value, axis, pairs)


def around_ring(value, axis, step):
    count = lax.axis_size(axis)
    return lax.ppermute(value, axis, [(i, (i + step) % count) for i in range(count)])


def swapped(value, axis, bit):
    count = lax.axis_size(axis)
    return lax.ppermute(value, axis, [(i, i ^ bit) for i in range(count)])


def column_pieces(coarse):
    own = [
        coarse,
        around_ring(coarse, "gx", -2),
        around_ring(coarse, "gx", 4),
        around_ring(coarse, "gx", 2),
    ]
    return own + [swapped(piece, "gx", 1) for piece in own]


def body(old_state, old_dest, refine, parent_block, coarse_state, force):
    gx = lax.axis_index("gx")
    outgoing = stage(old_dest[0], old_state.reshape(SLOTS, PATCH_ROWS, CELLS))
    arrived = lax.all_to_all(outgoing, "gy", split_axis=0, concat_axis=0, tiled=True)
    coarse = coarse_state.reshape(2, PATCH_ROWS, CELLS)
    kept = swapped(swapped(keep(force, coarse), "gx", 1), "gx", 1)
    pieces = [kept.reshape(KEPT, PATCH_ROWS, CELLS)] + column_pieces(coarse)[1:]
    holder = parent_block[0, :1] >> 3
    owner = (((holder >> 1) - (gx >> 1)) & 3) + 4 * ((holder ^ gx) & 1)
    source, fresh, left, right, rows = outline(
        refine[0], parent_block[0], owner, arrived, pieces
    )
    depth, inner = interior(source, arrived, fresh, force)
    from_left = moved(right, "gy", 1)
    from_right = moved(left, "gy", -1)
    top, bottom, side = edges(rows, from_left, from_right)
    above = moved(bottom, "gx", 1)
    below = moved(top, "gx", -1)
    velocity = sweeps(inner, side, above, below)
    return depth, velocity


def solution(mesh):
    return jax.shard_map(
        body,
        mesh=mesh,
        in_specs=(
            P("gx", "gy", None, None, None),
            P("gx", "gy"),
            P("gx", "gy"),
            P("gx", "gy"),
            P("gx", "gy", None, None, None),
            P(None, "gx", "gy"),
        ),
        out_specs=(P("gx", "gy"), P(None, "gx", "gy")),
        check_vma=False,
    )
```

```python
import functools

import jax
import jax.numpy as jnp
from jax import lax
from jax.experimental import pallas as pl
from jax.experimental.pallas import tpu as pltpu
from jax.sharding import PartitionSpec as P

CELLS = 128
FIELDS = 3
SWEEPS = 6
SLOTS = 8
PEERS = 16
OWNERS = 8
REFINED = 2
HALO = 8
WIDTH = SLOTS * CELLS
PATCH_ROWS = FIELDS * CELLS
CHUNK_ROWS = PATCH_ROWS + HALO
EXT_ROWS = CELLS + 2 * HALO
TILES = EXT_ROWS // 8
BLOCKS = SLOTS + 1
EXT_COLS = BLOCKS * CELLS
OMEGA = 0.8
TIME_STEP = 0.5

MIB = 1024 * 1024
in_vmem = pl.BlockSpec(memory_space=pltpu.VMEM)
in_smem = pl.BlockSpec(memory_space=pltpu.SMEM)
in_hbm = pl.BlockSpec(memory_space=pltpu.HBM)
in_any = pl.BlockSpec(memory_space=pl.ANY)


def params(mib):
    return pltpu.CompilerParams(vmem_limit_bytes=mib * MIB)


def stage_kernel(dest, old, out, patch_v, note_v, in_sems, out_sems, note_sem):
    for slot in range(SLOTS):
        pltpu.make_async_copy(old.at[slot], patch_v.at[slot], in_sems.at[slot]).start()
    note_v[...] = jnp.full(note_v.shape, -1.0, jnp.float32)
    for slot in range(SLOTS):
        target = dest[slot]

        @pl.when(target >= 0)
        def _(target=target):
            where = lax.convert_element_type(target & (SLOTS - 1), jnp.float32)
            note_v[target >> 3] = jnp.full((HALO, CELLS), where, jnp.float32)

    notes = pltpu.make_async_copy(note_v, out.at[:, pl.ds(PATCH_ROWS, HALO)], note_sem)
    notes.start()

    def send(slot):
        rows = out.at[dest[slot] >> 3, pl.ds(0, PATCH_ROWS)]
        return pltpu.make_async_copy(patch_v.at[slot], rows, out_sems.at[slot])

    for slot in range(SLOTS):
        pltpu.make_async_copy(old.at[slot], patch_v.at[slot], in_sems.at[slot]).wait()

        @pl.when(dest[slot] >= 0)
        def _(slot=slot):
            send(slot).start()

    for slot in range(SLOTS):

        @pl.when(dest[slot] >= 0)
        def _(slot=slot):
            send(slot).wait()

    notes.wait()


def stage(dest, old):
    return pl.pallas_call(
        stage_kernel,
        out_shape=jax.ShapeDtypeStruct((PEERS, CHUNK_ROWS, CELLS), jnp.float32),
        in_specs=[in_smem, in_hbm],
        out_specs=in_any,
        scratch_shapes=[
            pltpu.VMEM((SLOTS, PATCH_ROWS, CELLS), jnp.float32),
            pltpu.VMEM((PEERS, HALO, CELLS), jnp.float32),
            pltpu.SemaphoreType.DMA((SLOTS,)),
            pltpu.SemaphoreType.DMA((SLOTS,)),
            pltpu.SemaphoreType.DMA,
        ],
        compiler_params=params(60),
        name="stage_outgoing",
    )(dest, old)


KEPT = 4
COLS_AT = 2 * PATCH_ROWS
ROWS_AT = COLS_AT + 4 * CELLS


def keep_kernel(force, coarse, out, kept_v, sems, out_sem):
    copies = [(coarse.at[0], 0, PATCH_ROWS), (coarse.at[1], PATCH_ROWS, PATCH_ROWS)]
    for field in range(2):
        for edge in range(2):
            number = field * 2 + edge
            cols = pl.ds(edge * (WIDTH - CELLS), CELLS)
            copies.append((force.at[field, :, cols], COLS_AT + number * CELLS, CELLS))
            for slot in range(SLOTS):
                part = force.at[field, pl.ds(edge * (CELLS - HALO), HALO), pl.ds(slot * CELLS, CELLS)]
                copies.append((part, ROWS_AT + (number * SLOTS + slot) * HALO, HALO))
    copies = [
        pltpu.make_async_copy(part, kept_v.at[pl.ds(first, size)], sems.at[number])
        for number, (part, first, size) in enumerate(copies)
    ]
    for copy in copies:
        copy.start()
    for copy in copies:
        copy.wait()
    last = pltpu.make_async_copy(kept_v, out, out_sem)
    last.start()
    last.wait()


def keep(force, coarse):
    shape = (KEPT * PATCH_ROWS, CELLS)
    return pl.pallas_call(
        keep_kernel,
        out_shape=jax.ShapeDtypeStruct(shape, jnp.float32),
        in_specs=[in_any] * 2,
        out_specs=in_any,
        scratch_shapes=[
            pltpu.VMEM(shape, jnp.float32),
            pltpu.SemaphoreType.DMA((6 + 4 * SLOTS,)),
            pltpu.SemaphoreType.DMA,
        ],
        compiler_params=params(24),
        cost_estimate=pl.CostEstimate(flops=1 << 18, bytes_accessed=3 << 20, transcendentals=0),
        name="keep_own",
    )(force, coarse)


def spread(quarter, fine_axis):
    fine = lax.broadcasted_iota(jnp.int32, (CELLS, CELLS), fine_axis)
    coarse = lax.broadcasted_iota(jnp.int32, (CELLS, CELLS), 1 - fine_axis)
    half = CELLS // 2
    middle = lax.shift_right_logical(fine, 1)
    beside = jnp.where((fine & 1) == 0, middle - 1, middle + 1)
    beside = jnp.clip(beside, 0, half - 1)
    base = quarter * half
    near = jnp.where(coarse == base + middle, 0.75, 0.0)
    far = jnp.where(coarse == base + beside, 0.25, 0.0)
    return (near + far).astype(jnp.bfloat16)


def split_two(value):
    high = value.astype(jnp.bfloat16)
    low = (value - high.astype(jnp.float32)).astype(jnp.bfloat16)
    return high, low


def dot(a, b):
    return jnp.dot(a, b, preferred_element_type=jnp.float32)


def outline_kernel(refine, code, owner, arrived, *refs):
    pieces, refs = refs[:OWNERS], refs[OWNERS:]
    source, fresh, sends, rows, parent_v, note_i, force_v, picks, sems, force_sem = refs
    odd_column = (lax.axis_index("gy") & 1) > 0
    force_copy = pltpu.make_async_copy(pieces[0].at[pl.ds(2, 2)], force_v, force_sem)
    force_copy.start()

    picks[0] = -1
    picks[1] = -1
    count = jnp.int32(0)
    for slot in range(SLOTS):
        here = refine[slot] > 0
        source[slot] = jnp.where(here, PEERS + count, 0)

        @pl.when(here)
        def _(slot=slot, count=count):
            picks[jnp.minimum(count, REFINED - 1)] = slot

        count = count + here.astype(jnp.int32)

    def quarter(piece, number, field):
        slot = picks[number]
        first = pl.multiple_of(field * CELLS + ((code[slot] >> 1) & 1) * (CELLS // 2), CELLS // 2)
        return pltpu.make_async_copy(
            piece.at[(code[slot] >> 2) & 1, pl.ds(first, CELLS // 2)],
            parent_v.at[number, field],
            sems.at[number],
        )

    for place, piece in enumerate(pieces):

        @pl.when(owner[0] == place)
        def _(piece=piece):
            for number in range(REFINED):

                @pl.when(picks[number] >= 0)
                def _(number=number):
                    for field in range(FIELDS):
                        quarter(piece, number, field).start()

    note_i[...] = arrived[:, PATCH_ROWS, :].astype(jnp.int32)
    for peer in range(PEERS):
        slot = note_i[peer, 0]

        @pl.when(slot >= 0)
        def _(slot=slot, peer=peer):
            source[slot] = peer

    def refined(number, _):
        @pl.when(picks[number] >= 0)
        def _():
            for field in range(FIELDS):
                quarter(pieces[0], number, field).wait()
            along_rows = spread(0, 0)[:, : CELLS // 2]
            along_cols = spread(code[picks[number]] & 1, 1)
            for field in range(FIELDS):
                high, low = split_two(parent_v[number, field])
                done = dot(along_rows, high) + dot(along_rows, low)
                high, low = split_two(done)
                at = slice(field * CELLS, (field + 1) * CELLS)
                fresh[number, at] = dot(high, along_cols) + dot(low, along_cols)

        return 0

    lax.fori_loop(0, REFINED, refined, 0)

    def taken(slot, first, size):
        origin = source[slot]
        kept = arrived[jnp.minimum(origin, PEERS - 1), first : first + size]
        new = fresh[jnp.clip(origin - PEERS, 0, REFINED - 1), first : first + size]
        return jnp.where(origin >= PEERS, new, kept)

    def forcing(first, size):
        part, first = divmod(first - COLS_AT, PATCH_ROWS)
        return TIME_STEP * force_v[part, first : first + size]

    force_copy.wait()
    for field in range(FIELDS):
        low = field * CELLS
        first = taken(0, low, CELLS)
        last = taken(SLOTS - 1, low, CELLS)
        if field > 0:
            first = first + forcing(COLS_AT + (2 * field - 2) * CELLS, CELLS)
            last = last + forcing(COLS_AT + (2 * field - 1) * CELLS, CELLS)
        left, right = first.T[:HALO], last.T[CELLS - HALO :]
        sends[0, field] = jnp.where(odd_column, left, right)
        sends[1, field] = jnp.where(odd_column, right, left)
        for slot in range(SLOTS):
            for edge, first in enumerate((low, low + CELLS - HALO)):
                value = taken(slot, first, HALO)
                if field > 0:
                    number = 2 * field - 2 + edge
                    value = value + forcing(ROWS_AT + (number * SLOTS + slot) * HALO, HALO)
                rows[edge, field, slot] = value


def outline(refine, code, owner, arrived, pieces):
    f32 = jnp.float32
    return pl.pallas_call(
        outline_kernel,
        out_shape=(
            jax.ShapeDtypeStruct((SLOTS,), jnp.int32),
            jax.ShapeDtypeStruct((REFINED, PATCH_ROWS, CELLS), f32),
            jax.ShapeDtypeStruct((2, FIELDS, HALO, CELLS), f32),
            jax.ShapeDtypeStruct((2, FIELDS, SLOTS, HALO, CELLS), f32),
        ),
        in_specs=[in_smem] * 3 + [in_vmem] + [in_any] * OWNERS,
        out_specs=[in_smem] + [in_vmem] * 3,
        scratch_shapes=[
            pltpu.VMEM((REFINED, FIELDS, CELLS // 2, CELLS), f32),
            pltpu.VMEM((PEERS, CELLS), jnp.int32),
            pltpu.VMEM((2, PATCH_ROWS, CELLS), f32),
            pltpu.SMEM((REFINED,), jnp.int32),
            pltpu.SemaphoreType.DMA((REFINED,)),
            pltpu.SemaphoreType.DMA,
        ],
        compiler_params=params(40),
        name="block_outline",
    )(refine, code, owner, arrived, *pieces)


def interior_kernel(source, arrived, fresh, force, depth, wide, force_v, force_sems, depth_sems):
    force_copies = [pltpu.make_async_copy(force.at[i], force_v.at[i], force_sems.at[i]) for i in range(2)]
    for copy in force_copies:
        copy.start()

    def depth_copy(slot):
        inner = wide.at[0, slot, pl.ds(HALO, CELLS)]
        cols = pl.ds(slot * CELLS, CELLS)
        return pltpu.make_async_copy(inner, depth.at[:, cols], depth_sems.at[slot])

    for field in range(FIELDS):
        if field > 0:
            force_copies[field - 1].wait()
        for slot in range(SLOTS):
            origin = source[slot]
            at = slice(field * CELLS, (field + 1) * CELLS)
            kept = arrived[jnp.minimum(origin, PEERS - 1), at]
            new = fresh[jnp.clip(origin - PEERS, 0, REFINED - 1), at]
            value = jnp.where(origin >= PEERS, new, kept)
            if field > 0:
                value = value + TIME_STEP * force_v[field - 1, :, slot * CELLS : (slot + 1) * CELLS]
            wide[field, slot, HALO : HALO + CELLS] = value
            if field == 0:
                depth_copy(slot).start()
    for slot in range(SLOTS):
        depth_copy(slot).wait()


def interior(source, arrived, fresh, force):
    f32 = jnp.float32
    return pl.pallas_call(
        interior_kernel,
        out_shape=(
            jax.ShapeDtypeStruct((CELLS, WIDTH), f32),
            jax.ShapeDtypeStruct((FIELDS, SLOTS, EXT_ROWS, CELLS), f32),
        ),
        in_specs=[in_smem] + [in_vmem] * 2 + [in_hbm],
        out_specs=[in_hbm, in_vmem],
        scratch_shapes=[
            pltpu.VMEM((2, CELLS, WIDTH), f32),
            pltpu.SemaphoreType.DMA((2,)),
            pltpu.SemaphoreType.DMA((SLOTS,)),
        ],
        compiler_params=params(24),
        cost_estimate=pl.CostEstimate(flops=1 << 20, bytes_accessed=6 << 20, transcendentals=0),
        name="block_interior",
    )(source, arrived, fresh, force)


def edge_kernel(rows, first, second, sends, side):
    odd_row, odd_column = (lax.axis_index("gx") & 1) > 0, (lax.axis_index("gy") & 1) > 0
    blank = jnp.zeros((CELLS - 2 * HALO, CELLS), jnp.float32)
    for field in range(FIELDS):
        one, two = first[field], second[field]
        from_right = jnp.where(odd_column, two, one)
        from_left = jnp.where(odd_column, one, two)
        tile = jnp.concatenate([from_right, blank, from_left], axis=0).T
        side[field, :HALO] = tile[:HALO]
        side[field, HALO : HALO + CELLS] = tile
        side[field, HALO + CELLS :] = tile[:HALO]
        for block in range(BLOCKS):
            if block < SLOTS:
                top, bottom = rows[0, field, block], rows[1, field, block]
            else:
                top, bottom = tile[:HALO], tile[CELLS - HALO :]
            at = slice(block * CELLS, (block + 1) * CELLS)
            sends[0, field, :, at] = jnp.where(odd_row, top, bottom)
            sends[1, field, :, at] = jnp.where(odd_row, bottom, top)


def edges(rows, first, second):
    f32 = jnp.float32
    return pl.pallas_call(
        edge_kernel,
        out_shape=(
            jax.ShapeDtypeStruct((2, FIELDS, HALO, EXT_COLS), f32),
            jax.ShapeDtypeStruct((FIELDS, EXT_ROWS, CELLS), f32),
        ),
        in_specs=[in_vmem] * 3,
        out_specs=[in_vmem] * 2,
        compiler_params=params(16),
        name="edge_rows",
    )(rows, first, second)


def sweep_kernel(inner, side, first, second, out, done_v, right, velo, faces, above, below, out_sems):
    row = lax.broadcasted_iota(jnp.int32, (8, EXT_COLS), 0)
    odd_row = (lax.axis_index("gx") & 1) > 0
    for field in range(FIELDS):
        one, two = first[field], second[field]
        above[field] = jnp.where(odd_row, one, two)
        below[field] = jnp.where(odd_row, two, one)

    def rows_of(t):
        return pl.ds(t, 8, stride=TILES)

    def spaced(field, t):
        parts = [inner[field, block, rows_of(t), :] for block in range(SLOTS)]
        value = jnp.concatenate(parts + [side[field, rows_of(t), :]], axis=1)
        if t < HALO:
            value = jnp.where(row == 0, above[field, t : t + 1, :], value)
        if t >= TILES - HALO:
            first = t - (TILES - HALO)
            value = jnp.where(row == 7, below[field, first : first + 1, :], value)
        return value

    def each_tile(load):
        first, last = load(0), load(TILES - 1)
        before, here = pltpu.roll(last, 1, 0), first
        for t in range(TILES):
            after = load(t + 1) if t < TILES - 1 else pltpu.roll(load(0), 7, 0)
            yield t, here, (before, after, pltpu.roll(here, 1, 1), pltpu.roll(here, EXT_COLS - 1, 1))
            before, here = here, after

    def weight(a, b):
        mean = (a + b) * 0.5
        return mean * mean * mean * (1.0 / 3.0)

    for t, here, others in each_tile(lambda t: spaced(0, t)):
        weights = [weight(here, other) for other in others]
        diagonal = here + weights[0] + weights[1] + weights[2] + weights[3]
        inside = here > 0.0
        scale = jnp.where(inside, OMEGA / jnp.where(inside, diagonal, 1.0), 0.0)
        for number, w in enumerate(weights):
            faces[number, t] = w * scale
        for field in range(2):
            start = spaced(field + 1, t) * scale
            right[field, t] = start
            velo[0, field, t] = start

    def relaxed(now, field, t, here, others):
        total = right[field, t] + (1.0 - OMEGA) * here
        for number, other in enumerate(others):
            total = total + faces[number, t] * other
        return total

    def step(s, _):
        now = s & 1
        for field in range(2):
            for t, here, others in each_tile(lambda t: velo[now, field, t]):
                velo[1 - now, field, t] = relaxed(now, field, t, here, others)
        return 0

    lax.fori_loop(0, SWEEPS - 2, step, 0)

    def out_copy(field, block):
        cols = pl.ds(block * CELLS, CELLS)
        source = done_v.at[field, block, pl.ds(HALO, CELLS)]
        return pltpu.make_async_copy(source, out.at[field, :, cols], out_sems.at[field, block])

    now = (SWEEPS - 2) % 2
    for field in range(2):
        for t, here, others in each_tile(lambda t: velo[now, field, t]):
            done = relaxed(now, field, t, here, others)
            for block in range(SLOTS):
                done_v[field, block, rows_of(t), :] = done[:, block * CELLS : (block + 1) * CELLS]
        for block in range(SLOTS):
            out_copy(field, block).start()
    for field in range(2):
        for block in range(SLOTS):
            out_copy(field, block).wait()


def sweeps(inner, side, first, second):
    f32 = jnp.float32
    tiles = (TILES, 8, EXT_COLS)
    return pl.pallas_call(
        sweep_kernel,
        out_shape=jax.ShapeDtypeStruct((2, CELLS, WIDTH), f32),
        in_specs=[in_vmem] * 4,
        out_specs=in_any,
        scratch_shapes=[
            pltpu.VMEM((2, SLOTS, EXT_ROWS, CELLS), f32),
            pltpu.VMEM((2,) + tiles, f32),
            pltpu.VMEM((2, 2) + tiles, f32),
            pltpu.VMEM((4,) + tiles, f32),
            pltpu.VMEM((FIELDS, HALO, EXT_COLS), f32),
            pltpu.VMEM((FIELDS, HALO, EXT_COLS), f32),
            pltpu.SemaphoreType.DMA((2, SLOTS)),
        ],
        compiler_params=params(40),
        name="jacobi_sweeps",
    )(inner, side, first, second)


def paired(value, axis, start):
    count = lax.axis_size(axis)
    pairs = [(i, i + 1) for i in range(start, count - 1, 2)]
    return lax.ppermute(value, axis, pairs + [(j, i) for i, j in pairs])


def around_ring(value, axis, step):
    count = lax.axis_size(axis)
    return lax.ppermute(value, axis, [(i, (i + step) % count) for i in range(count)])


def swapped(value, axis, bit):
    count = lax.axis_size(axis)
    return lax.ppermute(value, axis, [(i, i ^ bit) for i in range(count)])


def column_pieces(coarse):
    own = [
        coarse,
        around_ring(coarse, "gx", -2),
        around_ring(coarse, "gx", 4),
        around_ring(coarse, "gx", 2),
    ]
    return own + [swapped(piece, "gx", 1) for piece in own]


def body(old_state, old_dest, refine, parent_block, coarse_state, force):
    outgoing = stage(old_dest[0], old_state.reshape(SLOTS, PATCH_ROWS, CELLS))
    arrived = lax.all_to_all(outgoing, "gy", split_axis=0, concat_axis=0, tiled=True)
    coarse = coarse_state.reshape(2, PATCH_ROWS, CELLS)
    kept = swapped(swapped(keep(force, coarse), "gx", 1), "gx", 1)
    pieces = [kept.reshape(KEPT, PATCH_ROWS, CELLS)] + column_pieces(coarse)[1:]
    gx = lax.axis_index("gx")
    holder = parent_block[0, :1] >> 3
    owner = (((holder >> 1) - (gx >> 1)) & 3) + 4 * ((holder ^ gx) & 1)
    source, fresh, sends, rows = outline(refine[0], parent_block[0], owner, arrived, pieces)
    depth, inner = interior(source, arrived, fresh, force)
    first, second = paired(sends[0], "gy", 0), paired(sends[1], "gy", 1)
    sends, side = edges(rows, first, second)
    first, second = paired(sends[0], "gx", 0), paired(sends[1], "gx", 1)
    velocity = sweeps(inner, side, first, second)
    return depth, velocity


def solution(mesh):
    return jax.shard_map(
        body,
        mesh=mesh,
        in_specs=(
            P("gx", "gy", None, None, None),
            P("gx", "gy"),
            P("gx", "gy"),
            P("gx", "gy"),
            P("gx", "gy", None, None, None),
            P(None, "gx", "gy"),
        ),
        out_specs=(P("gx", "gy"), P(None, "gx", "gy")),
        check_vma=False,
    )
```

```python
import functools

import jax
import jax.numpy as jnp
from jax import lax
from jax.experimental import pallas as pl
from jax.experimental.pallas import tpu as pltpu
from jax.sharding import PartitionSpec as P

CELLS = 128
FIELDS = 3
SWEEPS = 6
SLOTS = 8
PEERS = 16
OWNERS = 8
REFINED = 2
HALO = 8
WIDTH = SLOTS * CELLS
PATCH_ROWS = FIELDS * CELLS
CHUNK_ROWS = PATCH_ROWS + HALO
EXT_ROWS = CELLS + 2 * HALO
TILES = EXT_ROWS // 8
BLOCKS = SLOTS + 1
EXT_COLS = BLOCKS * CELLS
OMEGA = 0.8
TIME_STEP = 0.5

MIB = 1024 * 1024
in_vmem = pl.BlockSpec(memory_space=pltpu.VMEM)
in_smem = pl.BlockSpec(memory_space=pltpu.SMEM)
in_hbm = pl.BlockSpec(memory_space=pltpu.HBM)
in_any = pl.BlockSpec(memory_space=pl.ANY)


def params(mib):
    return pltpu.CompilerParams(vmem_limit_bytes=mib * MIB)


ORDER = (0, 1, 3, 2, 10, 11, 9, 8, 4, 5, 7, 6, 14, 15, 13, 12)


def chunk_of(device):
    high, low = device >> 2, device & 3
    high = ((high & 1) << 1) | (high >> 1)
    return (high << 2) | ((low ^ (low >> 1)) ^ ((high & 1) * 3))


def stage_kernel(dest, old, out, patch_v, note_v, in_sems, out_sems, note_sem):
    for slot in range(SLOTS):
        pltpu.make_async_copy(old.at[slot], patch_v.at[slot], in_sems.at[slot]).start()
    note_v[...] = jnp.full(note_v.shape, -1.0, jnp.float32)
    for slot in range(SLOTS):
        target = dest[slot]

        @pl.when(target >= 0)
        def _(target=target):
            where = lax.convert_element_type(target & (SLOTS - 1), jnp.float32)
            note_v[chunk_of(target >> 3)] = jnp.full((HALO, CELLS), where, jnp.float32)

    notes = pltpu.make_async_copy(note_v, out.at[:, pl.ds(PATCH_ROWS, HALO)], note_sem)
    notes.start()

    def send(slot):
        rows = out.at[chunk_of(dest[slot] >> 3), pl.ds(0, PATCH_ROWS)]
        return pltpu.make_async_copy(patch_v.at[slot], rows, out_sems.at[slot])

    for slot in range(SLOTS):
        pltpu.make_async_copy(old.at[slot], patch_v.at[slot], in_sems.at[slot]).wait()

        @pl.when(dest[slot] >= 0)
        def _(slot=slot):
            send(slot).start()

    for slot in range(SLOTS):

        @pl.when(dest[slot] >= 0)
        def _(slot=slot):
            send(slot).wait()

    notes.wait()


def stage(dest, old):
    return pl.pallas_call(
        stage_kernel,
        out_shape=jax.ShapeDtypeStruct((PEERS, CHUNK_ROWS, CELLS), jnp.float32),
        in_specs=[in_smem, in_hbm],
        out_specs=in_any,
        scratch_shapes=[
            pltpu.VMEM((SLOTS, PATCH_ROWS, CELLS), jnp.float32),
            pltpu.VMEM((PEERS, HALO, CELLS), jnp.float32),
            pltpu.SemaphoreType.DMA((SLOTS,)),
            pltpu.SemaphoreType.DMA((SLOTS,)),
            pltpu.SemaphoreType.DMA,
        ],
        compiler_params=params(60),
        name="stage_outgoing",
    )(dest, old)


KEPT = 4
COLS_AT = 2 * PATCH_ROWS
ROWS_AT = COLS_AT + 4 * CELLS


def keep_kernel(force, coarse, out, kept_v, sems, out_sem):
    copies = [(coarse.at[0], 0, PATCH_ROWS), (coarse.at[1], PATCH_ROWS, PATCH_ROWS)]
    for field in range(2):
        for edge in range(2):
            number = field * 2 + edge
            cols = pl.ds(edge * (WIDTH - CELLS), CELLS)
            copies.append((force.at[field, :, cols], COLS_AT + number * CELLS, CELLS))
            for slot in range(SLOTS):
                part = force.at[field, pl.ds(edge * (CELLS - HALO), HALO), pl.ds(slot * CELLS, CELLS)]
                copies.append((part, ROWS_AT + (number * SLOTS + slot) * HALO, HALO))
    copies = [
        pltpu.make_async_copy(part, kept_v.at[pl.ds(first, size)], sems.at[number])
        for number, (part, first, size) in enumerate(copies)
    ]
    for copy in copies:
        copy.start()
    for copy in copies:
        copy.wait()
    last = pltpu.make_async_copy(kept_v, out, out_sem)
    last.start()
    last.wait()


def keep(force, coarse):
    shape = (KEPT * PATCH_ROWS, CELLS)
    return pl.pallas_call(
        keep_kernel,
        out_shape=jax.ShapeDtypeStruct(shape, jnp.float32),
        in_specs=[in_any] * 2,
        out_specs=in_any,
        scratch_shapes=[
            pltpu.VMEM(shape, jnp.float32),
            pltpu.SemaphoreType.DMA((6 + 4 * SLOTS,)),
            pltpu.SemaphoreType.DMA,
        ],
        compiler_params=params(24),
        cost_estimate=pl.CostEstimate(flops=1 << 18, bytes_accessed=3 << 20, transcendentals=0),
        name="keep_own",
    )(force, coarse)


def spread(quarter, fine_axis):
    fine = lax.broadcasted_iota(jnp.int32, (CELLS, CELLS), fine_axis)
    coarse = lax.broadcasted_iota(jnp.int32, (CELLS, CELLS), 1 - fine_axis)
    half = CELLS // 2
    middle = lax.shift_right_logical(fine, 1)
    beside = jnp.where((fine & 1) == 0, middle - 1, middle + 1)
    beside = jnp.clip(beside, 0, half - 1)
    base = quarter * half
    near = jnp.where(coarse == base + middle, 0.75, 0.0)
    far = jnp.where(coarse == base + beside, 0.25, 0.0)
    return (near + far).astype(jnp.bfloat16)


def split_two(value):
    high = value.astype(jnp.bfloat16)
    low = (value - high.astype(jnp.float32)).astype(jnp.bfloat16)
    return high, low


def dot(a, b):
    return jnp.dot(a, b, preferred_element_type=jnp.float32)


def outline_kernel(refine, code, owner, arrived, *refs):
    pieces, refs = refs[:OWNERS], refs[OWNERS:]
    source, fresh, sends, rows, parent_v, note_i, force_v, picks, sems, force_sem = refs
    odd_column = (lax.axis_index("gy") & 1) > 0
    force_copy = pltpu.make_async_copy(pieces[0].at[pl.ds(2, 2)], force_v, force_sem)
    force_copy.start()

    picks[0] = -1
    picks[1] = -1
    count = jnp.int32(0)
    for slot in range(SLOTS):
        here = refine[slot] > 0
        source[slot] = jnp.where(here, PEERS + count, 0)

        @pl.when(here)
        def _(slot=slot, count=count):
            picks[jnp.minimum(count, REFINED - 1)] = slot

        count = count + here.astype(jnp.int32)

    def quarter(piece, number, field):
        slot = picks[number]
        first = pl.multiple_of(field * CELLS + ((code[slot] >> 1) & 1) * (CELLS // 2), CELLS // 2)
        return pltpu.make_async_copy(
            piece.at[(code[slot] >> 2) & 1, pl.ds(first, CELLS // 2)],
            parent_v.at[number, field],
            sems.at[number],
        )

    for place, piece in enumerate(pieces):

        @pl.when(owner[0] == place)
        def _(piece=piece):
            for number in range(REFINED):

                @pl.when(picks[number] >= 0)
                def _(number=number):
                    for field in range(FIELDS):
                        quarter(piece, number, field).start()

    note_i[...] = arrived[:, PATCH_ROWS, :].astype(jnp.int32)
    for peer in range(PEERS):
        slot = note_i[peer, 0]

        @pl.when(slot >= 0)
        def _(slot=slot, peer=peer):
            source[slot] = peer

    along_rows = jnp.concatenate([spread(0, 0)[:, : CELLS // 2]] * 2, axis=1)
    either = [jnp.concatenate([spread(side, 1)] * 2, axis=0) for side in range(2)]
    @pl.when(picks[0] >= 0)
    def _():
        for number in range(REFINED):

            @pl.when(picks[number] >= 0)
            def _(number=number):
                for field in range(FIELDS):
                    quarter(pieces[0], number, field).wait()

        for number in range(REFINED):
            side = code[jnp.maximum(picks[number], 0)] & 1
            along_cols = jnp.where(side > 0, either[1], either[0])
            parent = jnp.concatenate([parent_v[number, field] for field in range(FIELDS)], axis=1)
            done = dot(along_rows, jnp.concatenate(split_two(parent), axis=0))
            fields = [done[:, field * CELLS : (field + 1) * CELLS] for field in range(FIELDS)]
            done = jnp.concatenate(fields, axis=0)
            fresh[number] = dot(jnp.concatenate(split_two(done), axis=1), along_cols)

    def taken(slot, first, size):
        origin = source[slot]
        kept = arrived[jnp.minimum(origin, PEERS - 1), first : first + size]
        new = fresh[jnp.clip(origin - PEERS, 0, REFINED - 1), first : first + size]
        return jnp.where(origin >= PEERS, new, kept)

    def forcing(first, size):
        part, first = divmod(first - COLS_AT, PATCH_ROWS)
        return TIME_STEP * force_v[part, first : first + size]

    force_copy.wait()
    for field in range(FIELDS):
        low = field * CELLS
        first = taken(0, low, CELLS)
        last = taken(SLOTS - 1, low, CELLS)
        if field > 0:
            first = first + forcing(COLS_AT + (2 * field - 2) * CELLS, CELLS)
            last = last + forcing(COLS_AT + (2 * field - 1) * CELLS, CELLS)
        left, right = first.T[:HALO], last.T[CELLS - HALO :]
        sends[0, field] = jnp.where(odd_column, left, right)
        sends[1, field] = jnp.where(odd_column, right, left)
        for slot in range(SLOTS):
            for edge, first in enumerate((low, low + CELLS - HALO)):
                value = taken(slot, first, HALO)
                if field > 0:
                    number = 2 * field - 2 + edge
                    value = value + forcing(ROWS_AT + (number * SLOTS + slot) * HALO, HALO)
                rows[edge, field, slot] = value


def outline(refine, code, owner, arrived, pieces):
    f32 = jnp.float32
    return pl.pallas_call(
        outline_kernel,
        out_shape=(
            jax.ShapeDtypeStruct((SLOTS,), jnp.int32),
            jax.ShapeDtypeStruct((REFINED, PATCH_ROWS, CELLS), f32),
            jax.ShapeDtypeStruct((2, FIELDS, HALO, CELLS), f32),
            jax.ShapeDtypeStruct((2, FIELDS, SLOTS, HALO, CELLS), f32),
        ),
        in_specs=[in_smem] * 3 + [in_vmem] + [in_any] * OWNERS,
        out_specs=[in_smem] + [in_vmem] * 3,
        scratch_shapes=[
            pltpu.VMEM((REFINED, FIELDS, CELLS // 2, CELLS), f32),
            pltpu.VMEM((PEERS, CELLS), jnp.int32),
            pltpu.VMEM((2, PATCH_ROWS, CELLS), f32),
            pltpu.SMEM((REFINED,), jnp.int32),
            pltpu.SemaphoreType.DMA((REFINED,)),
            pltpu.SemaphoreType.DMA,
        ],
        compiler_params=params(40),
        name="block_outline",
    )(refine, code, owner, arrived, *pieces)


def interior_kernel(source, arrived, fresh, force, depth, wide, force_v, force_sems, depth_sems):
    force_copies = [pltpu.make_async_copy(force.at[i], force_v.at[i], force_sems.at[i]) for i in range(2)]
    for copy in force_copies:
        copy.start()

    def depth_copy(slot):
        inner = wide.at[0, slot, pl.ds(HALO, CELLS)]
        cols = pl.ds(slot * CELLS, CELLS)
        return pltpu.make_async_copy(inner, depth.at[:, cols], depth_sems.at[slot])

    for field in range(FIELDS):
        if field > 0:
            force_copies[field - 1].wait()
        for slot in range(SLOTS):
            origin = source[slot]
            at = slice(field * CELLS, (field + 1) * CELLS)
            kept = arrived[jnp.minimum(origin, PEERS - 1), at]
            new = fresh[jnp.clip(origin - PEERS, 0, REFINED - 1), at]
            value = jnp.where(origin >= PEERS, new, kept)
            if field > 0:
                value = value + TIME_STEP * force_v[field - 1, :, slot * CELLS : (slot + 1) * CELLS]
            wide[field, slot, HALO : HALO + CELLS] = value
            if field == 0:
                depth_copy(slot).start()
    for slot in range(SLOTS):
        depth_copy(slot).wait()


def interior(source, arrived, fresh, force):
    f32 = jnp.float32
    return pl.pallas_call(
        interior_kernel,
        out_shape=(
            jax.ShapeDtypeStruct((CELLS, WIDTH), f32),
            jax.ShapeDtypeStruct((FIELDS, SLOTS, EXT_ROWS, CELLS), f32),
        ),
        in_specs=[in_smem] + [in_vmem] * 2 + [in_hbm],
        out_specs=[in_hbm, in_vmem],
        scratch_shapes=[
            pltpu.VMEM((2, CELLS, WIDTH), f32),
            pltpu.SemaphoreType.DMA((2,)),
            pltpu.SemaphoreType.DMA((SLOTS,)),
        ],
        compiler_params=params(24),
        cost_estimate=pl.CostEstimate(flops=1 << 20, bytes_accessed=6 << 20, transcendentals=0),
        name="block_interior",
    )(source, arrived, fresh, force)


def edge_kernel(rows, first, second, sends, side):
    odd_row, odd_column = (lax.axis_index("gx") & 1) > 0, (lax.axis_index("gy") & 1) > 0
    blank = jnp.zeros((CELLS - 2 * HALO, CELLS), jnp.float32)
    for field in range(FIELDS):
        one, two = first[field], second[field]
        from_right = jnp.where(odd_column, two, one)
        from_left = jnp.where(odd_column, one, two)
        tile = jnp.concatenate([from_right, blank, from_left], axis=0).T
        side[field, :HALO] = tile[:HALO]
        side[field, HALO : HALO + CELLS] = tile
        side[field, HALO + CELLS :] = tile[:HALO]
        for block in range(BLOCKS):
            if block < SLOTS:
                top, bottom = rows[0, field, block], rows[1, field, block]
            else:
                top, bottom = tile[:HALO], tile[CELLS - HALO :]
            at = slice(block * CELLS, (block + 1) * CELLS)
            sends[0, field, :, at] = jnp.where(odd_row, top, bottom)
            sends[1, field, :, at] = jnp.where(odd_row, bottom, top)


def edges(rows, first, second):
    f32 = jnp.float32
    return pl.pallas_call(
        edge_kernel,
        out_shape=(
            jax.ShapeDtypeStruct((2, FIELDS, HALO, EXT_COLS), f32),
            jax.ShapeDtypeStruct((FIELDS, EXT_ROWS, CELLS), f32),
        ),
        in_specs=[in_vmem] * 3,
        out_specs=[in_vmem] * 2,
        compiler_params=params(16),
        name="edge_rows",
    )(rows, first, second)


def sweep_kernel(inner, side, first, second, out, done_v, right, velo, faces, above, below, out_sems):
    row = lax.broadcasted_iota(jnp.int32, (8, EXT_COLS), 0)
    odd_row = (lax.axis_index("gx") & 1) > 0
    for field in range(FIELDS):
        one, two = first[field], second[field]
        above[field] = jnp.where(odd_row, one, two)
        below[field] = jnp.where(odd_row, two, one)

    def rows_of(t):
        return pl.ds(t, 8, stride=TILES)

    def spaced(field, t):
        parts = [inner[field, block, rows_of(t), :] for block in range(SLOTS)]
        value = jnp.concatenate(parts + [side[field, rows_of(t), :]], axis=1)
        if t < HALO:
            value = jnp.where(row == 0, above[field, t : t + 1, :], value)
        if t >= TILES - HALO:
            first = t - (TILES - HALO)
            value = jnp.where(row == 7, below[field, first : first + 1, :], value)
        return value

    def each_tile(load):
        first, last = load(0), load(TILES - 1)
        before, here = pltpu.roll(last, 1, 0), first
        for t in range(TILES):
            after = load(t + 1) if t < TILES - 1 else pltpu.roll(load(0), 7, 0)
            yield t, here, (before, after, pltpu.roll(here, 1, 1), pltpu.roll(here, EXT_COLS - 1, 1))
            before, here = here, after

    def weight(a, b):
        mean = (a + b) * 0.5
        return mean * mean * mean * (1.0 / 3.0)

    for t, here, others in each_tile(lambda t: spaced(0, t)):
        weights = [weight(here, other) for other in others]
        diagonal = here + weights[0] + weights[1] + weights[2] + weights[3]
        inside = here > 0.0
        scale = jnp.where(inside, OMEGA / jnp.where(inside, diagonal, 1.0), 0.0)
        faces[0, t] = weights[1]
        faces[1, t] = weights[3]
        faces[2, t] = scale
        for field in range(2):
            start = spaced(field + 1, t) * scale
            right[field, t] = start
            velo[0, field, t] = start

    def relaxed(now, field):
        u = velo.at[now, field]
        last = faces[0, TILES - 1] * u[TILES - 1]
        above_flux = pltpu.roll(last, 1, 0)
        here = u[0]
        for t in range(TILES):
            after = u[t + 1] if t < TILES - 1 else pltpu.roll(u[0], 7, 0)
            south, east = faces[0, t], faces[1, t]
            flux = above_flux + south * after
            flux = flux + east * pltpu.roll(here, EXT_COLS - 1, 1)
            flux = flux + pltpu.roll(east * here, 1, 1)
            yield t, right[field, t] + (1.0 - OMEGA) * here + faces[2, t] * flux
            above_flux = south * here
            here = after

    def step(s, _):
        now = s & 1
        for field in range(2):
            for t, total in relaxed(now, field):
                velo[1 - now, field, t] = total
        return 0

    lax.fori_loop(0, SWEEPS - 2, step, 0)

    def out_copy(field, block):
        cols = pl.ds(block * CELLS, CELLS)
        source = done_v.at[field, block, pl.ds(HALO, CELLS)]
        return pltpu.make_async_copy(source, out.at[field, :, cols], out_sems.at[field, block])

    now = (SWEEPS - 2) % 2
    for field in range(2):
        for t, done in relaxed(now, field):
            for block in range(SLOTS):
                done_v[field, block, rows_of(t), :] = done[:, block * CELLS : (block + 1) * CELLS]
        for block in range(SLOTS):
            out_copy(field, block).start()
    for field in range(2):
        for block in range(SLOTS):
            out_copy(field, block).wait()


def sweeps(inner, side, first, second):
    f32 = jnp.float32
    tiles = (TILES, 8, EXT_COLS)
    return pl.pallas_call(
        sweep_kernel,
        out_shape=jax.ShapeDtypeStruct((2, CELLS, WIDTH), f32),
        in_specs=[in_vmem] * 4,
        out_specs=in_any,
        scratch_shapes=[
            pltpu.VMEM((2, SLOTS, EXT_ROWS, CELLS), f32),
            pltpu.VMEM((2,) + tiles, f32),
            pltpu.VMEM((2, 2) + tiles, f32),
            pltpu.VMEM((3,) + tiles, f32),
            pltpu.VMEM((FIELDS, HALO, EXT_COLS), f32),
            pltpu.VMEM((FIELDS, HALO, EXT_COLS), f32),
            pltpu.SemaphoreType.DMA((2, SLOTS)),
        ],
        compiler_params=params(40),
        name="jacobi_sweeps",
    )(inner, side, first, second)


def paired(value, axis, start):
    count = lax.axis_size(axis)
    pairs = [(i, i + 1) for i in range(start, count - 1, 2)]
    return lax.ppermute(value, axis, pairs + [(j, i) for i, j in pairs])


def around_ring(value, axis, step):
    count = lax.axis_size(axis)
    return lax.ppermute(value, axis, [(i, (i + step) % count) for i in range(count)])


def swapped(value, axis, bit):
    count = lax.axis_size(axis)
    return lax.ppermute(value, axis, [(i, i ^ bit) for i in range(count)])


def column_pieces(coarse):
    own = [
        coarse,
        around_ring(coarse, "gx", -2),
        around_ring(coarse, "gx", 4),
        around_ring(coarse, "gx", 2),
    ]
    return own + [swapped(piece, "gx", 1) for piece in own]


def body(old_state, old_dest, refine, parent_block, coarse_state, force):
    outgoing = stage(old_dest[0], old_state.reshape(SLOTS, PATCH_ROWS, CELLS))
    arrived = lax.all_to_all(
        outgoing, "gy", split_axis=0, concat_axis=0, tiled=True, axis_index_groups=[list(ORDER)]
    )
    coarse = coarse_state.reshape(2, PATCH_ROWS, CELLS)
    kept = swapped(swapped(keep(force, coarse), "gx", 1), "gx", 1)
    pieces = [kept.reshape(KEPT, PATCH_ROWS, CELLS)] + column_pieces(coarse)[1:]
    gx = lax.axis_index("gx")
    holder = parent_block[0, :1] >> 3
    owner = (((holder >> 1) - (gx >> 1)) & 3) + 4 * ((holder ^ gx) & 1)
    source, fresh, sends, rows = outline(refine[0], parent_block[0], owner, arrived, pieces)
    depth, inner = interior(source, arrived, fresh, force)
    first, second = paired(sends[0], "gy", 0), paired(sends[1], "gy", 1)
    sends, side = edges(rows, first, second)
    first, second = paired(sends[0], "gx", 0), paired(sends[1], "gx", 1)
    velocity = sweeps(inner, side, first, second)
    return depth, velocity


def solution(mesh):
    return jax.shard_map(
        body,
        mesh=mesh,
        in_specs=(
            P("gx", "gy", None, None, None),
            P("gx", "gy"),
            P("gx", "gy"),
            P("gx", "gy"),
            P("gx", "gy", None, None, None),
            P(None, "gx", "gy"),
        ),
        out_specs=(P("gx", "gy"), P(None, "gx", "gy")),
        check_vma=False,
    )
```

```python
import functools

import jax
import jax.numpy as jnp
from jax import lax
from jax.experimental import pallas as pl
from jax.experimental.pallas import tpu as pltpu
from jax.sharding import PartitionSpec as P

CELLS = 128
FIELDS = 3
SWEEPS = 6
SLOTS = 8
PEERS = 16
OWNERS = 8
REFINED = 2
HALO = 8
WIDTH = SLOTS * CELLS
PATCH_ROWS = FIELDS * CELLS
CHUNK_ROWS = PATCH_ROWS + HALO
EXT_ROWS = CELLS + 2 * HALO
TILES = EXT_ROWS // 8
BLOCKS = SLOTS + 1
EXT_COLS = BLOCKS * CELLS
OMEGA = 0.8
TIME_STEP = 0.5

MIB = 1024 * 1024
in_vmem = pl.BlockSpec(memory_space=pltpu.VMEM)
in_smem = pl.BlockSpec(memory_space=pltpu.SMEM)
in_hbm = pl.BlockSpec(memory_space=pltpu.HBM)
in_any = pl.BlockSpec(memory_space=pl.ANY)


def params(mib):
    return pltpu.CompilerParams(vmem_limit_bytes=mib * MIB)


ORDER = (0, 1, 3, 2, 10, 11, 9, 8, 4, 5, 7, 6, 14, 15, 13, 12)


def chunk_of(device):
    high, low = device >> 2, device & 3
    high = ((high & 1) << 1) | (high >> 1)
    return (high << 2) | ((low ^ (low >> 1)) ^ ((high & 1) * 3))


def stage_kernel(dest, old, out, patch_v, note_v, in_sems, out_sems, note_sem):
    for slot in range(SLOTS):
        pltpu.make_async_copy(old.at[slot], patch_v.at[slot], in_sems.at[slot]).start()
    note_v[...] = jnp.full(note_v.shape, -1.0, jnp.float32)
    for slot in range(SLOTS):
        target = dest[slot]

        @pl.when(target >= 0)
        def _(target=target):
            where = lax.convert_element_type(target & (SLOTS - 1), jnp.float32)
            note_v[chunk_of(target >> 3)] = jnp.full((HALO, CELLS), where, jnp.float32)

    notes = pltpu.make_async_copy(note_v, out.at[:, pl.ds(PATCH_ROWS, HALO)], note_sem)
    notes.start()

    def send(slot):
        rows = out.at[chunk_of(dest[slot] >> 3), pl.ds(0, PATCH_ROWS)]
        return pltpu.make_async_copy(patch_v.at[slot], rows, out_sems.at[slot])

    for slot in range(SLOTS):
        pltpu.make_async_copy(old.at[slot], patch_v.at[slot], in_sems.at[slot]).wait()

        @pl.when(dest[slot] >= 0)
        def _(slot=slot):
            send(slot).start()

    for slot in range(SLOTS):

        @pl.when(dest[slot] >= 0)
        def _(slot=slot):
            send(slot).wait()

    notes.wait()


def stage(dest, old):
    return pl.pallas_call(
        stage_kernel,
        out_shape=jax.ShapeDtypeStruct((PEERS, CHUNK_ROWS, CELLS), jnp.float32),
        in_specs=[in_smem, in_hbm],
        out_specs=in_any,
        scratch_shapes=[
            pltpu.VMEM((SLOTS, PATCH_ROWS, CELLS), jnp.float32),
            pltpu.VMEM((PEERS, HALO, CELLS), jnp.float32),
            pltpu.SemaphoreType.DMA((SLOTS,)),
            pltpu.SemaphoreType.DMA((SLOTS,)),
            pltpu.SemaphoreType.DMA,
        ],
        compiler_params=params(60),
        name="stage_outgoing",
    )(dest, old)


KEPT = 4
COLS_AT = 2 * PATCH_ROWS
ROWS_AT = COLS_AT + 4 * CELLS


def keep_kernel(force, coarse, out, kept_v, sems, out_sem):
    copies = [(coarse.at[0], 0, PATCH_ROWS), (coarse.at[1], PATCH_ROWS, PATCH_ROWS)]
    for field in range(2):
        for edge in range(2):
            number = field * 2 + edge
            cols = pl.ds(edge * (WIDTH - CELLS), CELLS)
            copies.append((force.at[field, :, cols], COLS_AT + number * CELLS, CELLS))
            for slot in range(SLOTS):
                part = force.at[field, pl.ds(edge * (CELLS - HALO), HALO), pl.ds(slot * CELLS, CELLS)]
                copies.append((part, ROWS_AT + (number * SLOTS + slot) * HALO, HALO))
    copies = [
        pltpu.make_async_copy(part, kept_v.at[pl.ds(first, size)], sems.at[number])
        for number, (part, first, size) in enumerate(copies)
    ]
    for copy in copies:
        copy.start()
    for copy in copies:
        copy.wait()
    last = pltpu.make_async_copy(kept_v, out, out_sem)
    last.start()
    last.wait()


def keep(force, coarse):
    shape = (KEPT * PATCH_ROWS, CELLS)
    return pl.pallas_call(
        keep_kernel,
        out_shape=jax.ShapeDtypeStruct(shape, jnp.float32),
        in_specs=[in_any] * 2,
        out_specs=in_any,
        scratch_shapes=[
            pltpu.VMEM(shape, jnp.float32),
            pltpu.SemaphoreType.DMA((6 + 4 * SLOTS,)),
            pltpu.SemaphoreType.DMA,
        ],
        compiler_params=params(24),
        cost_estimate=pl.CostEstimate(flops=1 << 18, bytes_accessed=3 << 20, transcendentals=0),
        name="keep_own",
    )(force, coarse)


def spread(quarter, fine_axis):
    fine = lax.broadcasted_iota(jnp.int32, (CELLS, CELLS), fine_axis)
    coarse = lax.broadcasted_iota(jnp.int32, (CELLS, CELLS), 1 - fine_axis)
    half = CELLS // 2
    middle = lax.shift_right_logical(fine, 1)
    beside = jnp.where((fine & 1) == 0, middle - 1, middle + 1)
    beside = jnp.clip(beside, 0, half - 1)
    base = quarter * half
    near = jnp.where(coarse == base + middle, 0.75, 0.0)
    far = jnp.where(coarse == base + beside, 0.25, 0.0)
    return (near + far).astype(jnp.bfloat16)


def split_two(value):
    high = value.astype(jnp.bfloat16)
    low = (value - high.astype(jnp.float32)).astype(jnp.bfloat16)
    return high, low


def dot(a, b):
    return jnp.dot(a, b, preferred_element_type=jnp.float32)


def outline_kernel(refine, code, owner, arrived, *refs):
    pieces, refs = refs[:OWNERS], refs[OWNERS:]
    source, fresh, sends, rows, parent_v, note_i, force_v, picks, sems, force_sem = refs
    odd_column = (lax.axis_index("gy") & 1) > 0
    force_copy = pltpu.make_async_copy(pieces[0].at[pl.ds(2, 2)], force_v, force_sem)
    force_copy.start()

    picks[0] = -1
    picks[1] = -1
    count = jnp.int32(0)
    for slot in range(SLOTS):
        here = refine[slot] > 0
        source[slot] = jnp.where(here, PEERS + count, 0)

        @pl.when(here)
        def _(slot=slot, count=count):
            picks[jnp.minimum(count, REFINED - 1)] = slot

        count = count + here.astype(jnp.int32)

    def quarter(piece, number, field):
        slot = picks[number]
        first = pl.multiple_of(field * CELLS + ((code[slot] >> 1) & 1) * (CELLS // 2), CELLS // 2)
        return pltpu.make_async_copy(
            piece.at[(code[slot] >> 2) & 1, pl.ds(first, CELLS // 2)],
            parent_v.at[number, field],
            sems.at[number],
        )

    for place, piece in enumerate(pieces):

        @pl.when(owner[0] == place)
        def _(piece=piece):
            for number in range(REFINED):

                @pl.when(picks[number] >= 0)
                def _(number=number):
                    for field in range(FIELDS):
                        quarter(piece, number, field).start()

    note_i[...] = arrived[:, PATCH_ROWS, :].astype(jnp.int32)
    for peer in range(PEERS):
        slot = note_i[peer, 0]

        @pl.when(slot >= 0)
        def _(slot=slot, peer=peer):
            source[slot] = peer

    along_rows = jnp.concatenate([spread(0, 0)[:, : CELLS // 2]] * 2, axis=1)
    either = [jnp.concatenate([spread(side, 1)] * 2, axis=0) for side in range(2)]
    @pl.when(picks[0] >= 0)
    def _():
        for number in range(REFINED):

            @pl.when(picks[number] >= 0)
            def _(number=number):
                for field in range(FIELDS):
                    quarter(pieces[0], number, field).wait()

        for number in range(REFINED):
            side = code[jnp.maximum(picks[number], 0)] & 1
            along_cols = jnp.where(side > 0, either[1], either[0])
            parent = jnp.concatenate([parent_v[number, field] for field in range(FIELDS)], axis=1)
            done = dot(along_rows, jnp.concatenate(split_two(parent), axis=0))
            fields = [done[:, field * CELLS : (field + 1) * CELLS] for field in range(FIELDS)]
            done = jnp.concatenate(fields, axis=0)
            fresh[number] = dot(jnp.concatenate(split_two(done), axis=1), along_cols)

    def taken(slot, first, size):
        origin = source[slot]
        kept = arrived[jnp.minimum(origin, PEERS - 1), first : first + size]
        new = fresh[jnp.clip(origin - PEERS, 0, REFINED - 1), first : first + size]
        return jnp.where(origin >= PEERS, new, kept)

    def forcing(first, size):
        part, first = divmod(first - COLS_AT, PATCH_ROWS)
        return TIME_STEP * force_v[part, first : first + size]

    force_copy.wait()
    for field in range(FIELDS):
        low = field * CELLS
        first = taken(0, low, CELLS)
        last = taken(SLOTS - 1, low, CELLS)
        if field > 0:
            first = first + forcing(COLS_AT + (2 * field - 2) * CELLS, CELLS)
            last = last + forcing(COLS_AT + (2 * field - 1) * CELLS, CELLS)
        left, right = first.T[:HALO], last.T[CELLS - HALO :]
        sends[0, field] = jnp.where(odd_column, left, right)
        sends[1, field] = jnp.where(odd_column, right, left)
        for slot in range(SLOTS):
            for edge, first in enumerate((low, low + CELLS - HALO)):
                value = taken(slot, first, HALO)
                if field > 0:
                    number = 2 * field - 2 + edge
                    value = value + forcing(ROWS_AT + (number * SLOTS + slot) * HALO, HALO)
                rows[edge, field, slot] = value


def outline(refine, code, owner, arrived, pieces):
    f32 = jnp.float32
    return pl.pallas_call(
        outline_kernel,
        out_shape=(
            jax.ShapeDtypeStruct((SLOTS,), jnp.int32),
            jax.ShapeDtypeStruct((REFINED, PATCH_ROWS, CELLS), f32),
            jax.ShapeDtypeStruct((2, FIELDS, HALO, CELLS), f32),
            jax.ShapeDtypeStruct((2, FIELDS, SLOTS, HALO, CELLS), f32),
        ),
        in_specs=[in_smem] * 3 + [in_vmem] + [in_any] * OWNERS,
        out_specs=[in_smem] + [in_vmem] * 3,
        scratch_shapes=[
            pltpu.VMEM((REFINED, FIELDS, CELLS // 2, CELLS), f32),
            pltpu.VMEM((PEERS, CELLS), jnp.int32),
            pltpu.VMEM((2, PATCH_ROWS, CELLS), f32),
            pltpu.SMEM((REFINED,), jnp.int32),
            pltpu.SemaphoreType.DMA((REFINED,)),
            pltpu.SemaphoreType.DMA,
        ],
        compiler_params=params(40),
        name="block_outline",
    )(refine, code, owner, arrived, *pieces)


def interior_kernel(source, arrived, fresh, force, depth, wide, force_v, force_sems, depth_sems):
    force_copies = [pltpu.make_async_copy(force.at[i], force_v.at[i], force_sems.at[i]) for i in range(2)]
    for copy in force_copies:
        copy.start()

    def depth_copy(slot):
        inner = wide.at[0, slot, pl.ds(HALO, CELLS)]
        cols = pl.ds(slot * CELLS, CELLS)
        return pltpu.make_async_copy(inner, depth.at[:, cols], depth_sems.at[slot])

    for field in range(FIELDS):
        if field > 0:
            force_copies[field - 1].wait()
        for slot in range(SLOTS):
            origin = source[slot]
            at = slice(field * CELLS, (field + 1) * CELLS)
            kept = arrived[jnp.minimum(origin, PEERS - 1), at]
            new = fresh[jnp.clip(origin - PEERS, 0, REFINED - 1), at]
            value = jnp.where(origin >= PEERS, new, kept)
            if field > 0:
                value = value + TIME_STEP * force_v[field - 1, :, slot * CELLS : (slot + 1) * CELLS]
            wide[field, slot, HALO : HALO + CELLS] = value
            if field == 0:
                depth_copy(slot).start()
    for slot in range(SLOTS):
        depth_copy(slot).wait()


def interior(source, arrived, fresh, force):
    f32 = jnp.float32
    return pl.pallas_call(
        interior_kernel,
        out_shape=(
            jax.ShapeDtypeStruct((CELLS, WIDTH), f32),
            jax.ShapeDtypeStruct((FIELDS, SLOTS, EXT_ROWS, CELLS), f32),
        ),
        in_specs=[in_smem] + [in_vmem] * 2 + [in_hbm],
        out_specs=[in_hbm, in_vmem],
        scratch_shapes=[
            pltpu.VMEM((2, CELLS, WIDTH), f32),
            pltpu.SemaphoreType.DMA((2,)),
            pltpu.SemaphoreType.DMA((SLOTS,)),
        ],
        compiler_params=params(24),
        cost_estimate=pl.CostEstimate(flops=1 << 20, bytes_accessed=6 << 20, transcendentals=0),
        name="block_interior",
    )(source, arrived, fresh, force)


def edge_kernel(rows, second, first, sends, side):
    odd_row, odd_column = (lax.axis_index("gx") & 1) > 0, (lax.axis_index("gy") & 1) > 0
    blank = jnp.zeros((CELLS - 2 * HALO, CELLS), jnp.float32)
    for field in range(FIELDS):
        one, two = first[field], second[field]
        from_right = jnp.where(odd_column, two, one)
        from_left = jnp.where(odd_column, one, two)
        tile = jnp.concatenate([from_right, blank, from_left], axis=0).T
        side[field, :HALO] = tile[:HALO]
        side[field, HALO : HALO + CELLS] = tile
        side[field, HALO + CELLS :] = tile[:HALO]
        for block in range(BLOCKS):
            if block < SLOTS:
                top, bottom = rows[0, field, block], rows[1, field, block]
            else:
                top, bottom = tile[:HALO], tile[CELLS - HALO :]
            at = slice(block * CELLS, (block + 1) * CELLS)
            sends[0, field, :, at] = jnp.where(odd_row, top, bottom)
            sends[1, field, :, at] = jnp.where(odd_row, bottom, top)


def edges(rows, second, first):
    f32 = jnp.float32
    return pl.pallas_call(
        edge_kernel,
        out_shape=(
            jax.ShapeDtypeStruct((2, FIELDS, HALO, EXT_COLS), f32),
            jax.ShapeDtypeStruct((FIELDS, EXT_ROWS, CELLS), f32),
        ),
        in_specs=[in_vmem] * 3,
        out_specs=[in_vmem] * 2,
        compiler_params=params(16),
        name="edge_rows",
    )(rows, second, first)


def sweep_kernel(inner, side, second, first, out, done_v, right, velo, faces, above, below, out_sems):
    row = lax.broadcasted_iota(jnp.int32, (8, EXT_COLS), 0)
    odd_row = (lax.axis_index("gx") & 1) > 0
    for field in range(FIELDS):
        one, two = first[field], second[field]
        above[field] = jnp.where(odd_row, one, two)
        below[field] = jnp.where(odd_row, two, one)

    def rows_of(t):
        return pl.ds(t, 8, stride=TILES)

    def spaced(field, t):
        parts = [inner[field, block, rows_of(t), :] for block in range(SLOTS)]
        value = jnp.concatenate(parts + [side[field, rows_of(t), :]], axis=1)
        if t < HALO:
            value = jnp.where(row == 0, above[field, t : t + 1, :], value)
        if t >= TILES - HALO:
            first = t - (TILES - HALO)
            value = jnp.where(row == 7, below[field, first : first + 1, :], value)
        return value

    def each_tile(load):
        first, last = load(0), load(TILES - 1)
        before, here = pltpu.roll(last, 1, 0), first
        for t in range(TILES):
            after = load(t + 1) if t < TILES - 1 else pltpu.roll(load(0), 7, 0)
            yield t, here, (before, after, pltpu.roll(here, 1, 1), pltpu.roll(here, EXT_COLS - 1, 1))
            before, here = here, after

    def weight(a, b):
        mean = (a + b) * 0.5
        return mean * mean * mean * (1.0 / 3.0)

    for t, here, others in each_tile(lambda t: spaced(0, t)):
        weights = [weight(here, other) for other in others]
        diagonal = here + weights[0] + weights[1] + weights[2] + weights[3]
        inside = here > 0.0
        scale = jnp.where(inside, OMEGA / jnp.where(inside, diagonal, 1.0), 0.0)
        faces[0, t] = weights[1]
        faces[1, t] = weights[3]
        faces[2, t] = scale
        for field in range(2):
            start = spaced(field + 1, t) * scale
            right[field, t] = start
            velo[0, field, t] = start

    def relaxed(now, field):
        u = velo.at[now, field]
        last = faces[0, TILES - 1] * u[TILES - 1]
        above_flux = pltpu.roll(last, 1, 0)
        here = u[0]
        for t in range(TILES):
            after = u[t + 1] if t < TILES - 1 else pltpu.roll(u[0], 7, 0)
            south, east = faces[0, t], faces[1, t]
            flux = above_flux + south * after
            flux = flux + east * pltpu.roll(here, EXT_COLS - 1, 1)
            flux = flux + pltpu.roll(east * here, 1, 1)
            yield t, right[field, t] + (1.0 - OMEGA) * here + faces[2, t] * flux
            above_flux = south * here
            here = after

    def step(s, _):
        now = s & 1
        for field in range(2):
            for t, total in relaxed(now, field):
                velo[1 - now, field, t] = total
        return 0

    lax.fori_loop(0, SWEEPS - 2, step, 0)

    def out_copy(field, block):
        cols = pl.ds(block * CELLS, CELLS)
        source = done_v.at[field, block, pl.ds(HALO, CELLS)]
        return pltpu.make_async_copy(source, out.at[field, :, cols], out_sems.at[field, block])

    now = (SWEEPS - 2) % 2
    for field in range(2):
        for t, done in relaxed(now, field):
            for block in range(SLOTS):
                done_v[field, block, rows_of(t), :] = done[:, block * CELLS : (block + 1) * CELLS]
        for block in range(SLOTS):
            out_copy(field, block).start()
    for field in range(2):
        for block in range(SLOTS):
            out_copy(field, block).wait()


def sweeps(inner, side, second, first):
    f32 = jnp.float32
    tiles = (TILES, 8, EXT_COLS)
    return pl.pallas_call(
        sweep_kernel,
        out_shape=jax.ShapeDtypeStruct((2, CELLS, WIDTH), f32),
        in_specs=[in_vmem] * 4,
        out_specs=in_any,
        scratch_shapes=[
            pltpu.VMEM((2, SLOTS, EXT_ROWS, CELLS), f32),
            pltpu.VMEM((2,) + tiles, f32),
            pltpu.VMEM((2, 2) + tiles, f32),
            pltpu.VMEM((3,) + tiles, f32),
            pltpu.VMEM((FIELDS, HALO, EXT_COLS), f32),
            pltpu.VMEM((FIELDS, HALO, EXT_COLS), f32),
            pltpu.SemaphoreType.DMA((2, SLOTS)),
        ],
        compiler_params=params(40),
        name="jacobi_sweeps",
    )(inner, side, second, first)


def paired(value, axis, start):
    count = lax.axis_size(axis)
    pairs = [(i, i + 1) for i in range(start, count - 1, 2)]
    return lax.ppermute(value, axis, pairs + [(j, i) for i, j in pairs])


def around_ring(value, axis, step):
    count = lax.axis_size(axis)
    return lax.ppermute(value, axis, [(i, (i + step) % count) for i in range(count)])


def swapped(value, axis, bit):
    count = lax.axis_size(axis)
    return lax.ppermute(value, axis, [(i, i ^ bit) for i in range(count)])


def column_pieces(coarse):
    own = [
        coarse,
        around_ring(coarse, "gx", -2),
        around_ring(coarse, "gx", 4),
        around_ring(coarse, "gx", 2),
    ]
    return own + [swapped(piece, "gx", 1) for piece in own]


def body(old_state, old_dest, refine, parent_block, coarse_state, force):
    outgoing = stage(old_dest[0], old_state.reshape(SLOTS, PATCH_ROWS, CELLS))
    arrived = lax.all_to_all(
        outgoing, "gy", split_axis=0, concat_axis=0, tiled=True, axis_index_groups=[list(ORDER)]
    )
    coarse = coarse_state.reshape(2, PATCH_ROWS, CELLS)
    kept = swapped(swapped(keep(force, coarse), "gx", 1), "gx", 1)
    pieces = [kept.reshape(KEPT, PATCH_ROWS, CELLS)] + column_pieces(coarse)[1:]
    gx = lax.axis_index("gx")
    holder = parent_block[0, :1] >> 3
    owner = (((holder >> 1) - (gx >> 1)) & 3) + 4 * ((holder ^ gx) & 1)
    source, fresh, sends, rows = outline(refine[0], parent_block[0], owner, arrived, pieces)
    depth, inner = interior(source, arrived, fresh, force)
    second = paired(sends[1], "gy", 1)
    first = paired(sends[0], "gy", 0)
    sends, side = edges(rows, second, first)
    second = paired(sends[1], "gx", 1)
    first = paired(sends[0], "gx", 0)
    velocity = sweeps(inner, side, second, first)
    return depth, velocity


def solution(mesh):
    return jax.shard_map(
        body,
        mesh=mesh,
        in_specs=(
            P("gx", "gy", None, None, None),
            P("gx", "gy"),
            P("gx", "gy"),
            P("gx", "gy"),
            P("gx", "gy", None, None, None),
            P(None, "gx", "gy"),
        ),
        out_specs=(P("gx", "gy"), P(None, "gx", "gy")),
        check_vma=False,
    )
```

```python
import functools

import jax
import jax.numpy as jnp
from jax import lax
from jax.experimental import pallas as pl
from jax.experimental.pallas import tpu as pltpu
from jax.sharding import PartitionSpec as P

CELLS = 128
FIELDS = 3
SWEEPS = 6
SLOTS = 8
PEERS = 16
OWNERS = 8
REFINED = 2
HALO = 8
WIDTH = SLOTS * CELLS
PATCH_ROWS = FIELDS * CELLS
CHUNK_ROWS = PATCH_ROWS + HALO
EXT_ROWS = CELLS + 2 * HALO
TILES = EXT_ROWS // 8
BLOCKS = SLOTS + 1
EXT_COLS = BLOCKS * CELLS
OMEGA = 0.8
TIME_STEP = 0.5

MIB = 1024 * 1024
in_vmem = pl.BlockSpec(memory_space=pltpu.VMEM)
in_smem = pl.BlockSpec(memory_space=pltpu.SMEM)
in_hbm = pl.BlockSpec(memory_space=pltpu.HBM)
in_any = pl.BlockSpec(memory_space=pl.ANY)


def params(mib):
    return pltpu.CompilerParams(vmem_limit_bytes=mib * MIB)


ORDER = (13, 15, 14, 6, 7, 5, 4, 8, 9, 11, 10, 2, 3, 1, 0, 12)


def chunk_of(device):
    place = jnp.int32(0)
    for number, other in enumerate(ORDER):
        place = jnp.where(device == other, number, place)
    return place


def stage_kernel(dest, old, out, patch_v, note_v, in_sems, out_sems, note_sem):
    for slot in range(SLOTS):
        pltpu.make_async_copy(old.at[slot], patch_v.at[slot], in_sems.at[slot]).start()
    note_v[...] = jnp.full(note_v.shape, -1.0, jnp.float32)
    for slot in range(SLOTS):
        target = dest[slot]

        @pl.when(target >= 0)
        def _(target=target):
            where = lax.convert_element_type(target & (SLOTS - 1), jnp.float32)
            note_v[chunk_of(target >> 3)] = jnp.full((HALO, CELLS), where, jnp.float32)

    notes = pltpu.make_async_copy(note_v, out.at[:, pl.ds(PATCH_ROWS, HALO)], note_sem)
    notes.start()

    def send(slot):
        rows = out.at[chunk_of(dest[slot] >> 3), pl.ds(0, PATCH_ROWS)]
        return pltpu.make_async_copy(patch_v.at[slot], rows, out_sems.at[slot])

    for slot in range(SLOTS):
        pltpu.make_async_copy(old.at[slot], patch_v.at[slot], in_sems.at[slot]).wait()

        @pl.when(dest[slot] >= 0)
        def _(slot=slot):
            send(slot).start()

    for slot in range(SLOTS):

        @pl.when(dest[slot] >= 0)
        def _(slot=slot):
            send(slot).wait()

    notes.wait()


def stage(dest, old):
    return pl.pallas_call(
        stage_kernel,
        out_shape=jax.ShapeDtypeStruct((PEERS, CHUNK_ROWS, CELLS), jnp.float32),
        in_specs=[in_smem, in_hbm],
        out_specs=in_any,
        scratch_shapes=[
            pltpu.VMEM((SLOTS, PATCH_ROWS, CELLS), jnp.float32),
            pltpu.VMEM((PEERS, HALO, CELLS), jnp.float32),
            pltpu.SemaphoreType.DMA((SLOTS,)),
            pltpu.SemaphoreType.DMA((SLOTS,)),
            pltpu.SemaphoreType.DMA,
        ],
        compiler_params=params(60),
        name="stage_outgoing",
    )(dest, old)


KEPT = 4
COLS_AT = 2 * PATCH_ROWS
ROWS_AT = COLS_AT + 4 * CELLS


def keep_kernel(force, coarse, out, kept_v, sems, out_sem):
    copies = [(coarse.at[0], 0, PATCH_ROWS), (coarse.at[1], PATCH_ROWS, PATCH_ROWS)]
    for field in range(2):
        for edge in range(2):
            number = field * 2 + edge
            cols = pl.ds(edge * (WIDTH - CELLS), CELLS)
            copies.append((force.at[field, :, cols], COLS_AT + number * CELLS, CELLS))
            for slot in range(SLOTS):
                part = force.at[field, pl.ds(edge * (CELLS - HALO), HALO), pl.ds(slot * CELLS, CELLS)]
                copies.append((part, ROWS_AT + (number * SLOTS + slot) * HALO, HALO))
    copies = [
        pltpu.make_async_copy(part, kept_v.at[pl.ds(first, size)], sems.at[number])
        for number, (part, first, size) in enumerate(copies)
    ]
    for copy in copies:
        copy.start()
    for copy in copies:
        copy.wait()
    last = pltpu.make_async_copy(kept_v, out, out_sem)
    last.start()
    last.wait()


def keep(force, coarse):
    shape = (KEPT * PATCH_ROWS, CELLS)
    return pl.pallas_call(
        keep_kernel,
        out_shape=jax.ShapeDtypeStruct(shape, jnp.float32),
        in_specs=[in_any] * 2,
        out_specs=in_any,
        scratch_shapes=[
            pltpu.VMEM(shape, jnp.float32),
            pltpu.SemaphoreType.DMA((6 + 4 * SLOTS,)),
            pltpu.SemaphoreType.DMA,
        ],
        compiler_params=params(24),
        cost_estimate=pl.CostEstimate(flops=1 << 18, bytes_accessed=3 << 20, transcendentals=0),
        name="keep_own",
    )(force, coarse)


def spread(quarter, fine_axis):
    fine = lax.broadcasted_iota(jnp.int32, (CELLS, CELLS), fine_axis)
    coarse = lax.broadcasted_iota(jnp.int32, (CELLS, CELLS), 1 - fine_axis)
    half = CELLS // 2
    middle = lax.shift_right_logical(fine, 1)
    beside = jnp.where((fine & 1) == 0, middle - 1, middle + 1)
    beside = jnp.clip(beside, 0, half - 1)
    base = quarter * half
    near = jnp.where(coarse == base + middle, 0.75, 0.0)
    far = jnp.where(coarse == base + beside, 0.25, 0.0)
    return (near + far).astype(jnp.bfloat16)


def split_two(value):
    high = value.astype(jnp.bfloat16)
    low = (value - high.astype(jnp.float32)).astype(jnp.bfloat16)
    return high, low


def dot(a, b):
    return jnp.dot(a, b, preferred_element_type=jnp.float32)


def outline_kernel(refine, code, owner, arrived, *refs):
    pieces, refs = refs[:OWNERS], refs[OWNERS:]
    source, fresh, sends, rows, parent_v, note_i, force_v, picks, sems, force_sem = refs
    odd_column = (lax.axis_index("gy") & 1) > 0
    force_copy = pltpu.make_async_copy(pieces[0].at[pl.ds(2, 2)], force_v, force_sem)
    force_copy.start()

    picks[0] = -1
    picks[1] = -1
    count = jnp.int32(0)
    for slot in range(SLOTS):
        here = refine[slot] > 0
        source[slot] = jnp.where(here, PEERS + count, 0)

        @pl.when(here)
        def _(slot=slot, count=count):
            picks[jnp.minimum(count, REFINED - 1)] = slot

        count = count + here.astype(jnp.int32)

    def quarter(piece, number, field):
        slot = picks[number]
        first = pl.multiple_of(field * CELLS + ((code[slot] >> 1) & 1) * (CELLS // 2), CELLS // 2)
        return pltpu.make_async_copy(
            piece.at[(code[slot] >> 2) & 1, pl.ds(first, CELLS // 2)],
            parent_v.at[number, field],
            sems.at[number],
        )

    for place, piece in enumerate(pieces):

        @pl.when(owner[0] == place)
        def _(piece=piece):
            for number in range(REFINED):

                @pl.when(picks[number] >= 0)
                def _(number=number):
                    for field in range(FIELDS):
                        quarter(piece, number, field).start()

    note_i[...] = arrived[:, PATCH_ROWS, :].astype(jnp.int32)
    for peer in range(PEERS):
        slot = note_i[peer, 0]

        @pl.when(slot >= 0)
        def _(slot=slot, peer=peer):
            source[slot] = peer

    along_rows = jnp.concatenate([spread(0, 0)[:, : CELLS // 2]] * 2, axis=1)
    either = [jnp.concatenate([spread(side, 1)] * 2, axis=0) for side in range(2)]
    @pl.when(picks[0] >= 0)
    def _():
        for number in range(REFINED):

            @pl.when(picks[number] >= 0)
            def _(number=number):
                for field in range(FIELDS):
                    quarter(pieces[0], number, field).wait()

        for number in range(REFINED):
            side = code[jnp.maximum(picks[number], 0)] & 1
            along_cols = jnp.where(side > 0, either[1], either[0])
            parent = jnp.concatenate([parent_v[number, field] for field in range(FIELDS)], axis=1)
            done = dot(along_rows, jnp.concatenate(split_two(parent), axis=0))
            fields = [done[:, field * CELLS : (field + 1) * CELLS] for field in range(FIELDS)]
            done = jnp.concatenate(fields, axis=0)
            fresh[number] = dot(jnp.concatenate(split_two(done), axis=1), along_cols)

    def taken(slot, first, size):
        origin = source[slot]
        kept = arrived[jnp.minimum(origin, PEERS - 1), first : first + size]
        new = fresh[jnp.clip(origin - PEERS, 0, REFINED - 1), first : first + size]
        return jnp.where(origin >= PEERS, new, kept)

    def forcing(first, size):
        part, first = divmod(first - COLS_AT, PATCH_ROWS)
        return TIME_STEP * force_v[part, first : first + size]

    force_copy.wait()
    for field in range(FIELDS):
        low = field * CELLS
        first = taken(0, low, CELLS)
        last = taken(SLOTS - 1, low, CELLS)
        if field > 0:
            first = first + forcing(COLS_AT + (2 * field - 2) * CELLS, CELLS)
            last = last + forcing(COLS_AT + (2 * field - 1) * CELLS, CELLS)
        left, right = first.T[:HALO], last.T[CELLS - HALO :]
        sends[0, field] = jnp.where(odd_column, left, right)
        sends[1, field] = jnp.where(odd_column, right, left)
        for slot in range(SLOTS):
            for edge, first in enumerate((low, low + CELLS - HALO)):
                value = taken(slot, first, HALO)
                if field > 0:
                    number = 2 * field - 2 + edge
                    value = value + forcing(ROWS_AT + (number * SLOTS + slot) * HALO, HALO)
                rows[edge, field, slot] = value


def outline(refine, code, owner, arrived, pieces):
    f32 = jnp.float32
    return pl.pallas_call(
        outline_kernel,
        out_shape=(
            jax.ShapeDtypeStruct((SLOTS,), jnp.int32),
            jax.ShapeDtypeStruct((REFINED, PATCH_ROWS, CELLS), f32),
            jax.ShapeDtypeStruct((2, FIELDS, HALO, CELLS), f32),
            jax.ShapeDtypeStruct((2, FIELDS, SLOTS, HALO, CELLS), f32),
        ),
        in_specs=[in_smem] * 3 + [in_vmem] + [in_any] * OWNERS,
        out_specs=[in_smem] + [in_vmem] * 3,
        scratch_shapes=[
            pltpu.VMEM((REFINED, FIELDS, CELLS // 2, CELLS), f32),
            pltpu.VMEM((PEERS, CELLS), jnp.int32),
            pltpu.VMEM((2, PATCH_ROWS, CELLS), f32),
            pltpu.SMEM((REFINED,), jnp.int32),
            pltpu.SemaphoreType.DMA((REFINED,)),
            pltpu.SemaphoreType.DMA,
        ],
        compiler_params=params(40),
        name="block_outline",
    )(refine, code, owner, arrived, *pieces)


def interior_kernel(source, arrived, fresh, force, depth, wide, force_v, force_sems, depth_sems):
    force_copies = [pltpu.make_async_copy(force.at[i], force_v.at[i], force_sems.at[i]) for i in range(2)]
    for copy in force_copies:
        copy.start()

    def depth_copy(slot):
        inner = wide.at[0, slot, pl.ds(HALO, CELLS)]
        cols = pl.ds(slot * CELLS, CELLS)
        return pltpu.make_async_copy(inner, depth.at[:, cols], depth_sems.at[slot])

    for field in range(FIELDS):
        if field > 0:
            force_copies[field - 1].wait()
        for slot in range(SLOTS):
            origin = source[slot]
            at = slice(field * CELLS, (field + 1) * CELLS)
            kept = arrived[jnp.minimum(origin, PEERS - 1), at]
            new = fresh[jnp.clip(origin - PEERS, 0, REFINED - 1), at]
            value = jnp.where(origin >= PEERS, new, kept)
            if field > 0:
                value = value + TIME_STEP * force_v[field - 1, :, slot * CELLS : (slot + 1) * CELLS]
            wide[field, slot, HALO : HALO + CELLS] = value
            if field == 0:
                depth_copy(slot).start()
    for slot in range(SLOTS):
        depth_copy(slot).wait()


def interior(source, arrived, fresh, force):
    f32 = jnp.float32
    return pl.pallas_call(
        interior_kernel,
        out_shape=(
            jax.ShapeDtypeStruct((CELLS, WIDTH), f32),
            jax.ShapeDtypeStruct((FIELDS, SLOTS, EXT_ROWS, CELLS), f32),
        ),
        in_specs=[in_smem] + [in_vmem] * 2 + [in_hbm],
        out_specs=[in_hbm, in_vmem],
        scratch_shapes=[
            pltpu.VMEM((2, CELLS, WIDTH), f32),
            pltpu.SemaphoreType.DMA((2,)),
            pltpu.SemaphoreType.DMA((SLOTS,)),
        ],
        compiler_params=params(24),
        cost_estimate=pl.CostEstimate(flops=1 << 20, bytes_accessed=6 << 20, transcendentals=0),
        name="block_interior",
    )(source, arrived, fresh, force)


def edge_kernel(rows, second, first, sends, side):
    odd_row, odd_column = (lax.axis_index("gx") & 1) > 0, (lax.axis_index("gy") & 1) > 0
    blank = jnp.zeros((CELLS - 2 * HALO, CELLS), jnp.float32)
    for field in range(FIELDS):
        one, two = first[field], second[field]
        from_right = jnp.where(odd_column, two, one)
        from_left = jnp.where(odd_column, one, two)
        tile = jnp.concatenate([from_right, blank, from_left], axis=0).T
        side[field, :HALO] = tile[:HALO]
        side[field, HALO : HALO + CELLS] = tile
        side[field, HALO + CELLS :] = tile[:HALO]
        for block in range(BLOCKS):
            if block < SLOTS:
                top, bottom = rows[0, field, block], rows[1, field, block]
            else:
                top, bottom = tile[:HALO], tile[CELLS - HALO :]
            at = slice(block * CELLS, (block + 1) * CELLS)
            sends[0, field, :, at] = jnp.where(odd_row, top, bottom)
            sends[1, field, :, at] = jnp.where(odd_row, bottom, top)


def edges(rows, second, first):
    f32 = jnp.float32
    return pl.pallas_call(
        edge_kernel,
        out_shape=(
            jax.ShapeDtypeStruct((2, FIELDS, HALO, EXT_COLS), f32),
            jax.ShapeDtypeStruct((FIELDS, EXT_ROWS, CELLS), f32),
        ),
        in_specs=[in_vmem] * 3,
        out_specs=[in_vmem] * 2,
        compiler_params=params(16),
        name="edge_rows",
    )(rows, second, first)


def sweep_kernel(inner, side, second, first, out, done_v, right, velo, faces, above, below, out_sems):
    row = lax.broadcasted_iota(jnp.int32, (8, EXT_COLS), 0)
    odd_row = (lax.axis_index("gx") & 1) > 0
    for field in range(FIELDS):
        one, two = first[field], second[field]
        above[field] = jnp.where(odd_row, one, two)
        below[field] = jnp.where(odd_row, two, one)

    def rows_of(t):
        return pl.ds(t, 8, stride=TILES)

    def spaced(field, t):
        parts = [inner[field, block, rows_of(t), :] for block in range(SLOTS)]
        value = jnp.concatenate(parts + [side[field, rows_of(t), :]], axis=1)
        if t < HALO:
            value = jnp.where(row == 0, above[field, t : t + 1, :], value)
        if t >= TILES - HALO:
            first = t - (TILES - HALO)
            value = jnp.where(row == 7, below[field, first : first + 1, :], value)
        return value

    def each_tile(load):
        first, last = load(0), load(TILES - 1)
        before, here = pltpu.roll(last, 1, 0), first
        for t in range(TILES):
            after = load(t + 1) if t < TILES - 1 else pltpu.roll(load(0), 7, 0)
            yield t, here, (before, after, pltpu.roll(here, 1, 1), pltpu.roll(here, EXT_COLS - 1, 1))
            before, here = here, after

    def weight(a, b):
        mean = (a + b) * 0.5
        return mean * mean * mean * (1.0 / 3.0)

    for t, here, others in each_tile(lambda t: spaced(0, t)):
        weights = [weight(here, other) for other in others]
        diagonal = here + weights[0] + weights[1] + weights[2] + weights[3]
        inside = here > 0.0
        scale = jnp.where(inside, OMEGA / jnp.where(inside, diagonal, 1.0), 0.0)
        faces[0, t] = weights[1]
        faces[1, t] = weights[3]
        faces[2, t] = scale
        for field in range(2):
            start = spaced(field + 1, t) * scale
            right[field, t] = start
            velo[0, field, t] = start

    def relaxed(now, field):
        u = velo.at[now, field]
        last = faces[0, TILES - 1] * u[TILES - 1]
        above_flux = pltpu.roll(last, 1, 0)
        here = u[0]
        for t in range(TILES):
            after = u[t + 1] if t < TILES - 1 else pltpu.roll(u[0], 7, 0)
            south, east = faces[0, t], faces[1, t]
            flux = above_flux + south * after
            flux = flux + east * pltpu.roll(here, EXT_COLS - 1, 1)
            flux = flux + pltpu.roll(east * here, 1, 1)
            yield t, right[field, t] + (1.0 - OMEGA) * here + faces[2, t] * flux
            above_flux = south * here
            here = after

    def step(s, _):
        now = s & 1
        for field in range(2):
            for t, total in relaxed(now, field):
                velo[1 - now, field, t] = total
        return 0

    lax.fori_loop(0, SWEEPS - 2, step, 0)

    def out_copy(field, block):
        cols = pl.ds(block * CELLS, CELLS)
        source = done_v.at[field, block, pl.ds(HALO, CELLS)]
        return pltpu.make_async_copy(source, out.at[field, :, cols], out_sems.at[field, block])

    now = (SWEEPS - 2) % 2
    for field in range(2):
        for t, done in relaxed(now, field):
            for block in range(SLOTS):
                done_v[field, block, rows_of(t), :] = done[:, block * CELLS : (block + 1) * CELLS]
        for block in range(SLOTS):
            out_copy(field, block).start()
    for field in range(2):
        for block in range(SLOTS):
            out_copy(field, block).wait()


def sweeps(inner, side, second, first):
    f32 = jnp.float32
    tiles = (TILES, 8, EXT_COLS)
    return pl.pallas_call(
        sweep_kernel,
        out_shape=jax.ShapeDtypeStruct((2, CELLS, WIDTH), f32),
        in_specs=[in_vmem] * 4,
        out_specs=in_any,
        scratch_shapes=[
            pltpu.VMEM((2, SLOTS, EXT_ROWS, CELLS), f32),
            pltpu.VMEM((2,) + tiles, f32),
            pltpu.VMEM((2, 2) + tiles, f32),
            pltpu.VMEM((3,) + tiles, f32),
            pltpu.VMEM((FIELDS, HALO, EXT_COLS), f32),
            pltpu.VMEM((FIELDS, HALO, EXT_COLS), f32),
            pltpu.SemaphoreType.DMA((2, SLOTS)),
        ],
        compiler_params=params(40),
        name="jacobi_sweeps",
    )(inner, side, second, first)


def paired(value, axis, start):
    count = lax.axis_size(axis)
    pairs = [(i, i + 1) for i in range(start, count - 1, 2)]
    return lax.ppermute(value, axis, pairs + [(j, i) for i, j in pairs])


def around_ring(value, axis, step):
    count = lax.axis_size(axis)
    return lax.ppermute(value, axis, [(i, (i + step) % count) for i in range(count)])


def swapped(value, axis, bit):
    count = lax.axis_size(axis)
    return lax.ppermute(value, axis, [(i, i ^ bit) for i in range(count)])


def column_pieces(coarse):
    own = [
        coarse,
        around_ring(coarse, "gx", -2),
        around_ring(coarse, "gx", 4),
        around_ring(coarse, "gx", 2),
    ]
    return own + [swapped(piece, "gx", 1) for piece in own]


def body(old_state, old_dest, refine, parent_block, coarse_state, force):
    outgoing = stage(old_dest[0], old_state.reshape(SLOTS, PATCH_ROWS, CELLS))
    arrived = lax.all_to_all(
        outgoing, "gy", split_axis=0, concat_axis=0, tiled=True, axis_index_groups=[list(ORDER)]
    )
    coarse = coarse_state.reshape(2, PATCH_ROWS, CELLS)
    kept = swapped(swapped(keep(force, coarse), "gx", 1), "gx", 1)
    pieces = [kept.reshape(KEPT, PATCH_ROWS, CELLS)] + column_pieces(coarse)[1:]
    gx = lax.axis_index("gx")
    holder = parent_block[0, :1] >> 3
    owner = (((holder >> 1) - (gx >> 1)) & 3) + 4 * ((holder ^ gx) & 1)
    source, fresh, sends, rows = outline(refine[0], parent_block[0], owner, arrived, pieces)
    depth, inner = interior(source, arrived, fresh, force)
    second = paired(sends[1], "gy", 1)
    first = paired(sends[0], "gy", 0)
    sends, side = edges(rows, second, first)
    second = paired(sends[1], "gx", 1)
    first = paired(sends[0], "gx", 0)
    velocity = sweeps(inner, side, second, first)
    return depth, velocity


def solution(mesh):
    return jax.shard_map(
        body,
        mesh=mesh,
        in_specs=(
            P("gx", "gy", None, None, None),
            P("gx", "gy"),
            P("gx", "gy"),
            P("gx", "gy"),
            P("gx", "gy", None, None, None),
            P(None, "gx", "gy"),
        ),
        out_specs=(P("gx", "gy"), P(None, "gx", "gy")),
        check_vma=False,
    )
```

```python
import functools

import jax
import jax.numpy as jnp
from jax import lax
from jax.experimental import pallas as pl
from jax.experimental.pallas import tpu as pltpu
from jax.sharding import PartitionSpec as P

CELLS = 128
FIELDS = 3
SWEEPS = 6
SLOTS = 8
PEERS = 16
OWNERS = 8
REFINED = 2
HALO = 8
WIDTH = SLOTS * CELLS
PATCH_ROWS = FIELDS * CELLS
CHUNK_ROWS = PATCH_ROWS + HALO
EXT_ROWS = CELLS + 2 * HALO
TILES = EXT_ROWS // 8
BLOCKS = SLOTS + 1
EXT_COLS = BLOCKS * CELLS
OMEGA = 0.8
TIME_STEP = 0.5

MIB = 1024 * 1024
in_vmem = pl.BlockSpec(memory_space=pltpu.VMEM)
in_smem = pl.BlockSpec(memory_space=pltpu.SMEM)
in_hbm = pl.BlockSpec(memory_space=pltpu.HBM)
in_any = pl.BlockSpec(memory_space=pl.ANY)


def params(mib):
    return pltpu.CompilerParams(vmem_limit_bytes=mib * MIB)


ORDER = (13, 15, 14, 6, 7, 5, 4, 8, 9, 11, 10, 2, 3, 1, 0, 12)


def chunk_of(device):
    place = jnp.int32(0)
    for number, other in enumerate(ORDER):
        place = jnp.where(device == other, number, place)
    return place


def stage_kernel(dest, old, out, patch_v, note_v, in_sems, out_sems, note_sem):
    for slot in range(SLOTS):
        pltpu.make_async_copy(old.at[slot], patch_v.at[slot], in_sems.at[slot]).start()
    note_v[...] = jnp.full(note_v.shape, -1.0, jnp.float32)
    for slot in range(SLOTS):
        target = dest[slot]

        @pl.when(target >= 0)
        def _(target=target):
            where = lax.convert_element_type(target & (SLOTS - 1), jnp.float32)
            note_v[chunk_of(target >> 3)] = jnp.full((HALO, CELLS), where, jnp.float32)

    notes = pltpu.make_async_copy(note_v, out.at[:, pl.ds(PATCH_ROWS, HALO)], note_sem)
    notes.start()

    def send(slot):
        rows = out.at[chunk_of(dest[slot] >> 3), pl.ds(0, PATCH_ROWS)]
        return pltpu.make_async_copy(patch_v.at[slot], rows, out_sems.at[slot])

    for slot in range(SLOTS):
        pltpu.make_async_copy(old.at[slot], patch_v.at[slot], in_sems.at[slot]).wait()

        @pl.when(dest[slot] >= 0)
        def _(slot=slot):
            send(slot).start()

    for slot in range(SLOTS):

        @pl.when(dest[slot] >= 0)
        def _(slot=slot):
            send(slot).wait()

    notes.wait()


def stage(dest, old):
    return pl.pallas_call(
        stage_kernel,
        out_shape=jax.ShapeDtypeStruct((PEERS, CHUNK_ROWS, CELLS), jnp.float32),
        in_specs=[in_smem, in_hbm],
        out_specs=in_any,
        scratch_shapes=[
            pltpu.VMEM((SLOTS, PATCH_ROWS, CELLS), jnp.float32),
            pltpu.VMEM((PEERS, HALO, CELLS), jnp.float32),
            pltpu.SemaphoreType.DMA((SLOTS,)),
            pltpu.SemaphoreType.DMA((SLOTS,)),
            pltpu.SemaphoreType.DMA,
        ],
        compiler_params=params(60),
        name="stage_outgoing",
    )(dest, old)


KEPT = 4
COLS_AT = 2 * PATCH_ROWS
ROWS_AT = COLS_AT + 4 * CELLS


def keep_kernel(force, coarse, out, kept_v, sems, out_sem):
    copies = [(coarse.at[0], 0, PATCH_ROWS), (coarse.at[1], PATCH_ROWS, PATCH_ROWS)]
    for field in range(2):
        for edge in range(2):
            number = field * 2 + edge
            cols = pl.ds(edge * (WIDTH - CELLS), CELLS)
            copies.append((force.at[field, :, cols], COLS_AT + number * CELLS, CELLS))
            for slot in range(SLOTS):
                part = force.at[field, pl.ds(edge * (CELLS - HALO), HALO), pl.ds(slot * CELLS, CELLS)]
                copies.append((part, ROWS_AT + (number * SLOTS + slot) * HALO, HALO))
    copies = [
        pltpu.make_async_copy(part, kept_v.at[pl.ds(first, size)], sems.at[number])
        for number, (part, first, size) in enumerate(copies)
    ]
    for copy in copies:
        copy.start()
    for copy in copies:
        copy.wait()
    last = pltpu.make_async_copy(kept_v, out, out_sem)
    last.start()
    last.wait()


def keep(force, coarse):
    shape = (KEPT * PATCH_ROWS, CELLS)
    return pl.pallas_call(
        keep_kernel,
        out_shape=jax.ShapeDtypeStruct(shape, jnp.float32),
        in_specs=[in_any] * 2,
        out_specs=in_any,
        scratch_shapes=[
            pltpu.VMEM(shape, jnp.float32),
            pltpu.SemaphoreType.DMA((6 + 4 * SLOTS,)),
            pltpu.SemaphoreType.DMA,
        ],
        compiler_params=params(24),
        cost_estimate=pl.CostEstimate(flops=1 << 18, bytes_accessed=3 << 20, transcendentals=0),
        name="keep_own",
    )(force, coarse)


def spread(quarter, fine_axis):
    fine = lax.broadcasted_iota(jnp.int32, (CELLS, CELLS), fine_axis)
    coarse = lax.broadcasted_iota(jnp.int32, (CELLS, CELLS), 1 - fine_axis)
    half = CELLS // 2
    middle = lax.shift_right_logical(fine, 1)
    beside = jnp.where((fine & 1) == 0, middle - 1, middle + 1)
    beside = jnp.clip(beside, 0, half - 1)
    base = quarter * half
    near = jnp.where(coarse == base + middle, 0.75, 0.0)
    far = jnp.where(coarse == base + beside, 0.25, 0.0)
    return (near + far).astype(jnp.bfloat16)


def split_two(value):
    high = value.astype(jnp.bfloat16)
    low = (value - high.astype(jnp.float32)).astype(jnp.bfloat16)
    return high, low


def dot(a, b):
    return jnp.dot(a, b, preferred_element_type=jnp.float32)


def outline_kernel(refine, code, owner, arrived, *refs):
    pieces, refs = refs[:OWNERS], refs[OWNERS:]
    source, fresh, sends, rows, parent_v, note_i, force_v, picks, sems, force_sem = refs
    odd_column = (lax.axis_index("gy") & 1) > 0
    force_copy = pltpu.make_async_copy(pieces[0].at[pl.ds(2, 2)], force_v, force_sem)
    force_copy.start()

    picks[0] = -1
    picks[1] = -1
    count = jnp.int32(0)
    for slot in range(SLOTS):
        here = refine[slot] > 0
        source[slot] = jnp.where(here, PEERS + count, 0)

        @pl.when(here)
        def _(slot=slot, count=count):
            picks[jnp.minimum(count, REFINED - 1)] = slot

        count = count + here.astype(jnp.int32)

    def quarter(piece, number, field):
        slot = picks[number]
        first = pl.multiple_of(field * CELLS + ((code[slot] >> 1) & 1) * (CELLS // 2), CELLS // 2)
        return pltpu.make_async_copy(
            piece.at[(code[slot] >> 2) & 1, pl.ds(first, CELLS // 2)],
            parent_v.at[number, field],
            sems.at[number],
        )

    for place, piece in enumerate(pieces):

        @pl.when(owner[0] == place)
        def _(piece=piece):
            for number in range(REFINED):

                @pl.when(picks[number] >= 0)
                def _(number=number):
                    for field in range(FIELDS):
                        quarter(piece, number, field).start()

    note_i[...] = arrived[:, PATCH_ROWS, :].astype(jnp.int32)
    for peer in range(PEERS):
        slot = note_i[peer, 0]

        @pl.when(slot >= 0)
        def _(slot=slot, peer=peer):
            source[slot] = peer

    along_rows = jnp.concatenate([spread(0, 0)[:, : CELLS // 2]] * 2, axis=1)
    either = [jnp.concatenate([spread(side, 1)] * 2, axis=0) for side in range(2)]
    @pl.when(picks[0] >= 0)
    def _():
        for number in range(REFINED):

            @pl.when(picks[number] >= 0)
            def _(number=number):
                for field in range(FIELDS):
                    quarter(pieces[0], number, field).wait()

        for number in range(REFINED):
            side = code[jnp.maximum(picks[number], 0)] & 1
            along_cols = jnp.where(side > 0, either[1], either[0])
            parent = jnp.concatenate([parent_v[number, field] for field in range(FIELDS)], axis=1)
            done = dot(along_rows, jnp.concatenate(split_two(parent), axis=0))
            fields = [done[:, field * CELLS : (field + 1) * CELLS] for field in range(FIELDS)]
            done = jnp.concatenate(fields, axis=0)
            fresh[number] = dot(jnp.concatenate(split_two(done), axis=1), along_cols)

    def taken(slot, first, size):
        origin = source[slot]
        kept = arrived[jnp.minimum(origin, PEERS - 1), first : first + size]
        new = fresh[jnp.clip(origin - PEERS, 0, REFINED - 1), first : first + size]
        return jnp.where(origin >= PEERS, new, kept)

    def forcing(first, size):
        part, first = divmod(first - COLS_AT, PATCH_ROWS)
        return TIME_STEP * force_v[part, first : first + size]

    force_copy.wait()
    for field in range(FIELDS):
        low = field * CELLS
        first = taken(0, low, CELLS)
        last = taken(SLOTS - 1, low, CELLS)
        if field > 0:
            first = first + forcing(COLS_AT + (2 * field - 2) * CELLS, CELLS)
            last = last + forcing(COLS_AT + (2 * field - 1) * CELLS, CELLS)
        left, right = first.T[:HALO], last.T[CELLS - HALO :]
        sends[0, field] = jnp.where(odd_column, left, right)
        sends[1, field] = jnp.where(odd_column, right, left)
        for slot in range(SLOTS):
            for edge, first in enumerate((low, low + CELLS - HALO)):
                value = taken(slot, first, HALO)
                if field > 0:
                    number = 2 * field - 2 + edge
                    value = value + forcing(ROWS_AT + (number * SLOTS + slot) * HALO, HALO)
                rows[edge, field, slot] = value


def outline(refine, code, owner, arrived, pieces):
    f32 = jnp.float32
    return pl.pallas_call(
        outline_kernel,
        out_shape=(
            jax.ShapeDtypeStruct((SLOTS,), jnp.int32),
            jax.ShapeDtypeStruct((REFINED, PATCH_ROWS, CELLS), f32),
            jax.ShapeDtypeStruct((2, FIELDS, HALO, CELLS), f32),
            jax.ShapeDtypeStruct((2, FIELDS, SLOTS, HALO, CELLS), f32),
        ),
        in_specs=[in_smem] * 3 + [in_vmem] + [in_any] * OWNERS,
        out_specs=[in_smem] + [in_vmem] * 3,
        scratch_shapes=[
            pltpu.VMEM((REFINED, FIELDS, CELLS // 2, CELLS), f32),
            pltpu.VMEM((PEERS, CELLS), jnp.int32),
            pltpu.VMEM((2, PATCH_ROWS, CELLS), f32),
            pltpu.SMEM((REFINED,), jnp.int32),
            pltpu.SemaphoreType.DMA((REFINED,)),
            pltpu.SemaphoreType.DMA,
        ],
        compiler_params=params(40),
        name="block_outline",
    )(refine, code, owner, arrived, *pieces)


def interior_kernel(source, arrived, fresh, force, depth, wide, force_v, force_sems, depth_sems):
    force_copies = [pltpu.make_async_copy(force.at[i], force_v.at[i], force_sems.at[i]) for i in range(2)]
    for copy in force_copies:
        copy.start()

    def depth_copy(slot):
        inner = wide.at[0, slot, pl.ds(HALO, CELLS)]
        cols = pl.ds(slot * CELLS, CELLS)
        return pltpu.make_async_copy(inner, depth.at[:, cols], depth_sems.at[slot])

    for field in range(FIELDS):
        if field > 0:
            force_copies[field - 1].wait()
        for slot in range(SLOTS):
            origin = source[slot]
            at = slice(field * CELLS, (field + 1) * CELLS)
            kept = arrived[jnp.minimum(origin, PEERS - 1), at]
            new = fresh[jnp.clip(origin - PEERS, 0, REFINED - 1), at]
            value = jnp.where(origin >= PEERS, new, kept)
            if field > 0:
                value = value + TIME_STEP * force_v[field - 1, :, slot * CELLS : (slot + 1) * CELLS]
            wide[field, slot, HALO : HALO + CELLS] = value
            if field == 0:
                depth_copy(slot).start()
    for slot in range(SLOTS):
        depth_copy(slot).wait()


def interior(source, arrived, fresh, force):
    f32 = jnp.float32
    return pl.pallas_call(
        interior_kernel,
        out_shape=(
            jax.ShapeDtypeStruct((CELLS, WIDTH), f32),
            jax.ShapeDtypeStruct((FIELDS, SLOTS, EXT_ROWS, CELLS), f32),
        ),
        in_specs=[in_smem] + [in_vmem] * 2 + [in_hbm],
        out_specs=[in_hbm, in_vmem],
        scratch_shapes=[
            pltpu.VMEM((2, CELLS, WIDTH), f32),
            pltpu.SemaphoreType.DMA((2,)),
            pltpu.SemaphoreType.DMA((SLOTS,)),
        ],
        compiler_params=params(24),
        cost_estimate=pl.CostEstimate(flops=1 << 20, bytes_accessed=6 << 20, transcendentals=0),
        name="block_interior",
    )(source, arrived, fresh, force)


def edge_kernel(rows, second, first, sends, side):
    odd_row, odd_column = (lax.axis_index("gx") & 1) > 0, (lax.axis_index("gy") & 1) > 0
    blank = jnp.zeros((CELLS - 2 * HALO, CELLS), jnp.float32)
    for field in range(FIELDS):
        one, two = first[field], second[field]
        from_right = jnp.where(odd_column, two, one)
        from_left = jnp.where(odd_column, one, two)
        tile = jnp.concatenate([from_right, blank, from_left], axis=0).T
        side[field, :HALO] = tile[:HALO]
        side[field, HALO : HALO + CELLS] = tile
        side[field, HALO + CELLS :] = tile[:HALO]
        for block in range(BLOCKS):
            if block < SLOTS:
                top, bottom = rows[0, field, block], rows[1, field, block]
            else:
                top, bottom = tile[:HALO], tile[CELLS - HALO :]
            at = slice(block * CELLS, (block + 1) * CELLS)
            sends[0, field, :, at] = jnp.where(odd_row, top, bottom)
            sends[1, field, :, at] = jnp.where(odd_row, bottom, top)


def edges(rows, second, first):
    f32 = jnp.float32
    return pl.pallas_call(
        edge_kernel,
        out_shape=(
            jax.ShapeDtypeStruct((2, FIELDS, HALO, EXT_COLS), f32),
            jax.ShapeDtypeStruct((FIELDS, EXT_ROWS, CELLS), f32),
        ),
        in_specs=[in_vmem] * 3,
        out_specs=[in_vmem] * 2,
        compiler_params=params(16),
        name="edge_rows",
    )(rows, second, first)


def sweep_kernel(inner, side, second, first, out, done_v, right, velo, faces, above, below, out_sems):
    row = lax.broadcasted_iota(jnp.int32, (8, EXT_COLS), 0)
    odd_row = (lax.axis_index("gx") & 1) > 0
    for field in range(FIELDS):
        one, two = first[field], second[field]
        above[field] = jnp.where(odd_row, one, two)
        below[field] = jnp.where(odd_row, two, one)

    def rows_of(t):
        return pl.ds(t, 8, stride=TILES)

    def spaced(field, t):
        parts = [inner[field, block, rows_of(t), :] for block in range(SLOTS)]
        value = jnp.concatenate(parts + [side[field, rows_of(t), :]], axis=1)
        if t < HALO:
            value = jnp.where(row == 0, above[field, t : t + 1, :], value)
        if t >= TILES - HALO:
            first = t - (TILES - HALO)
            value = jnp.where(row == 7, below[field, first : first + 1, :], value)
        return value

    def each_tile(load):
        first, last = load(0), load(TILES - 1)
        before, here = pltpu.roll(last, 1, 0), first
        for t in range(TILES):
            after = load(t + 1) if t < TILES - 1 else pltpu.roll(load(0), 7, 0)
            yield t, here, (before, after, pltpu.roll(here, 1, 1), pltpu.roll(here, EXT_COLS - 1, 1))
            before, here = here, after

    def weight(a, b):
        mean = (a + b) * 0.5
        return mean * mean * mean * (1.0 / 3.0)

    for t, here, others in each_tile(lambda t: spaced(0, t)):
        weights = [weight(here, other) for other in others]
        diagonal = here + weights[0] + weights[1] + weights[2] + weights[3]
        inside = here > 0.0
        scale = jnp.where(inside, OMEGA / jnp.where(inside, diagonal, 1.0), 0.0)
        faces[0, t] = weights[1]
        faces[1, t] = weights[3]
        faces[2, t] = scale
        for field in range(2):
            start = spaced(field + 1, t) * scale
            right[field, t] = start
            velo[0, field, t] = start

    def relaxed(now, field):
        u = velo.at[now, field]
        last = faces[0, TILES - 1] * u[TILES - 1]
        above_flux = pltpu.roll(last, 1, 0)
        here = u[0]
        for t in range(TILES):
            after = u[t + 1] if t < TILES - 1 else pltpu.roll(u[0], 7, 0)
            south, east = faces[0, t], faces[1, t]
            flux = above_flux + south * after
            flux = flux + east * pltpu.roll(here, EXT_COLS - 1, 1)
            flux = flux + pltpu.roll(east * here, 1, 1)
            yield t, right[field, t] + (1.0 - OMEGA) * here + faces[2, t] * flux
            above_flux = south * here
            here = after

    def step(s, _):
        now = s & 1
        for field in range(2):
            for t, total in relaxed(now, field):
                velo[1 - now, field, t] = total
        return 0

    lax.fori_loop(0, SWEEPS - 2, step, 0)

    def out_copy(field, block):
        cols = pl.ds(block * CELLS, CELLS)
        source = done_v.at[field, block, pl.ds(HALO, CELLS)]
        return pltpu.make_async_copy(source, out.at[field, :, cols], out_sems.at[field, block])

    now = (SWEEPS - 2) % 2
    for blocks in (range(SLOTS // 2), range(SLOTS // 2, SLOTS)):
        for field in range(2):
            for t, done in relaxed(now, field):
                for block in blocks:
                    done_v[field, block, rows_of(t), :] = done[:, block * CELLS : (block + 1) * CELLS]
            for block in blocks:
                out_copy(field, block).start()
    for field in range(2):
        for block in range(SLOTS):
            out_copy(field, block).wait()


def sweeps(inner, side, second, first):
    f32 = jnp.float32
    tiles = (TILES, 8, EXT_COLS)
    return pl.pallas_call(
        sweep_kernel,
        out_shape=jax.ShapeDtypeStruct((2, CELLS, WIDTH), f32),
        in_specs=[in_vmem] * 4,
        out_specs=in_any,
        scratch_shapes=[
            pltpu.VMEM((2, SLOTS, EXT_ROWS, CELLS), f32),
            pltpu.VMEM((2,) + tiles, f32),
            pltpu.VMEM((2, 2) + tiles, f32),
            pltpu.VMEM((3,) + tiles, f32),
            pltpu.VMEM((FIELDS, HALO, EXT_COLS), f32),
            pltpu.VMEM((FIELDS, HALO, EXT_COLS), f32),
            pltpu.SemaphoreType.DMA((2, SLOTS)),
        ],
        compiler_params=params(40),
        name="jacobi_sweeps",
    )(inner, side, second, first)


def paired(value, axis, start):
    count = lax.axis_size(axis)
    pairs = [(i, i + 1) for i in range(start, count - 1, 2)]
    return lax.ppermute(value, axis, pairs + [(j, i) for i, j in pairs])


def around_ring(value, axis, step):
    count = lax.axis_size(axis)
    return lax.ppermute(value, axis, [(i, (i + step) % count) for i in range(count)])


def swapped(value, axis, bit):
    count = lax.axis_size(axis)
    return lax.ppermute(value, axis, [(i, i ^ bit) for i in range(count)])


def column_pieces(coarse):
    own = [
        coarse,
        around_ring(coarse, "gx", -2),
        around_ring(coarse, "gx", 4),
        around_ring(coarse, "gx", 2),
    ]
    return own + [swapped(piece, "gx", 1) for piece in own]


def body(old_state, old_dest, refine, parent_block, coarse_state, force):
    outgoing = stage(old_dest[0], old_state.reshape(SLOTS, PATCH_ROWS, CELLS))
    arrived = lax.all_to_all(
        outgoing, "gy", split_axis=0, concat_axis=0, tiled=True, axis_index_groups=[list(ORDER)]
    )
    coarse = coarse_state.reshape(2, PATCH_ROWS, CELLS)
    kept = swapped(swapped(keep(force, coarse), "gx", 1), "gx", 1)
    pieces = [kept.reshape(KEPT, PATCH_ROWS, CELLS)] + column_pieces(coarse)[1:]
    gx = lax.axis_index("gx")
    holder = parent_block[0, :1] >> 3
    owner = (((holder >> 1) - (gx >> 1)) & 3) + 4 * ((holder ^ gx) & 1)
    source, fresh, sends, rows = outline(refine[0], parent_block[0], owner, arrived, pieces)
    depth, inner = interior(source, arrived, fresh, force)
    second = paired(sends[1], "gy", 1)
    first = paired(sends[0], "gy", 0)
    sends, side = edges(rows, second, first)
    second = paired(sends[1], "gx", 1)
    first = paired(sends[0], "gx", 0)
    velocity = sweeps(inner, side, second, first)
    return depth, velocity


def solution(mesh):
    return jax.shard_map(
        body,
        mesh=mesh,
        in_specs=(
            P("gx", "gy", None, None, None),
            P("gx", "gy"),
            P("gx", "gy"),
            P("gx", "gy"),
            P("gx", "gy", None, None, None),
            P(None, "gx", "gy"),
        ),
        out_specs=(P("gx", "gy"), P(None, "gx", "gy")),
        check_vma=False,
    )
```
